32 devices in a mesh: date: 2 (over x), blk: 8 (over z, y), sect: 2 (over core).
Axes of the slice: x: 2, y: 2, z: 4, core: 2. Of those that a mesh axis runs over, the one named last changes fastest.
Arguments:
- obs_weight: bfloat16 [16, 2, 512, 128], P(('date', 'blk'), 'sect'), parts along dimension 0, may hold values from -4 to 4
- obs_frac: bfloat16 [16, 2, 2, 512], P(('date', 'blk'), 'sect'), parts along dimension 0, may hold values from 0 to 1
- obs_cell: int32 [16, 2, 512], P(('date', 'blk'), 'sect'), parts along dimension 0, may hold values from 0 to 127
- obs_level: int32 [16, 2, 512], P(('date', 'blk'), 'sect'), parts along dimension 0, may hold values from 0 to 63
- obs_count: int32 [16, 2], P(('date', 'blk'), 'sect'), parts along dimension 0, may hold values from 1 to 512, as said below
- reach: int32 [16, 2], P(('date', 'blk')), parts along dimension 0, may hold values from 0 to 3, as said below
- length_x: float32 [64], replicated, may hold values from 0.5 to 2
- length_y: float32 [64], replicated, may hold values from 0.1 to 0.5
- tilt: float32 [64], replicated, may hold values from -0.7 to 0.7
- vert_len: float32 [64], replicated, may hold values from 1.5 to 12
- balance: float32 [64, 64], replicated, may hold values from -0.75 to 0.75
Outputs:
- increment: float32 [64, 2048, 128], P('sect', ('date', 'blk')), parts along dimension 1
The draws below stay inside these ranges and needn't reach their ends.
There are 2 independent parts, one for each index of `date`. The reference program is written for one: setup_inputs(seed, part) draws one part's arguments, and reference() takes and returns one part's arrays. A program takes and returns all parts, laid end to end along the dimension named above; an argument that names none is the same for every part. Nothing has to cross between parts.
Inputs may be any that keep to these rules, and one draw needn't show every extreme that they name: `obs_count`: 512 is reached in every draw. `reach`: 0 and 3 both occur in every draw.
All inputs are finite; a program needn't handle non-finite values.
Results may differ from the reference program's by a relative error of at most 0.0029.
Values may be sent and summed in bfloat16 or wider, within the bound.
A program may use at most 64 MiB of HBM per device.

```python
import math
import jax
import jax.numpy as jnp
from jax import lax

L = 64
C = 128
GX = 8
GY = 16
OBS_DEV = 512
REACH = 3
G_DEV = 128
BLOCKS = 8
SECTIONS = 2


def draw_obs_count(key, part):
    first_key, second_key = jax.random.split(jax.random.fold_in(key, 11))
    base_rows = jax.random.randint(first_key, (BLOCKS, SECTIONS), OBS_DEV // 16, OBS_DEV // 4 + 1)
    doublings = jax.random.randint(second_key, (BLOCKS, SECTIONS), 0, 3)
    counts = jnp.minimum(jnp.left_shift(base_rows, doublings), OBS_DEV)
    return counts.at[0, 0].set(OBS_DEV).astype(jnp.int32)


def draw_reach(key, part):
    spans = jax.random.randint(jax.random.fold_in(key, 23), (BLOCKS, 2), 0, REACH + 1)
    return spans.at[0, 0].set(REACH).at[0, 1].set(0).astype(jnp.int32)


def place_ends(array, rng, smallest, top_value):
    dims = array.shape
    index_at = [jax.random.randint(jax.random.fold_in(rng, axis), (), 0, dims[axis]) for axis in range(len(dims))]
    array = array.at[tuple(index_at)].set(smallest)
    longest = dims.index(max(dims))
    index_at[longest] = (index_at[longest] + 1) % dims[longest]
    return array.at[tuple(index_at)].set(top_value)


def levels(own_key, shape, cuts, smallest, high):
    gain = 1.0
    for dim, parts in cuts:
        steps = jax.random.uniform(jax.random.fold_in(jax.random.fold_in(own_key, 6), dim), (parts,), jnp.float32, smallest / len(cuts), high / len(cuts))
        gain = gain * jnp.repeat(jnp.exp(steps), shape[dim] // parts).reshape((-1,) + (1,) * (len(shape) - 1 - dim))
    return gain


def scatter_about(key, dims, deviation, most, shards=(), held_as=jnp.bfloat16):
    loudness = levels(key, dims, shards, -0.22, 0.18) if shards else 1.0
    drawn = jax.random.normal(key, dims, jnp.float32) * deviation * loudness
    return jnp.minimum(jnp.maximum(drawn, -most), most).astype(held_as)


def setup_inputs(seed: int = 0, part: int = 0) -> dict:
    key_of = jax.random.split(jax.random.key(seed), 12)
    part_keys = jax.random.split(jax.random.fold_in(key_of[11], part), 12)
    return {
        "obs_weight": scatter_about(part_keys[0], (BLOCKS, SECTIONS, OBS_DEV, C), 0.5, 4.0, ((0, 8), (1, 2))),
        "obs_frac": jnp.clip(1.0 * jax.random.uniform(part_keys[1], (BLOCKS, SECTIONS, 2, OBS_DEV), jnp.float32) ** levels(part_keys[1], (BLOCKS, SECTIONS, 2, OBS_DEV), ((0, 8), (1, 2)), -0.2, 0.2), 0.0, 1.0).astype(jnp.bfloat16),
        "obs_cell": place_ends(jax.random.randint(part_keys[2], (BLOCKS, SECTIONS, OBS_DEV), 0, G_DEV), jax.random.fold_in(part_keys[2], 1), 0, G_DEV - 1).astype(jnp.int32),
        "obs_level": place_ends(jax.random.randint(part_keys[3], (BLOCKS, SECTIONS, OBS_DEV), 0, L), jax.random.fold_in(part_keys[3], 1), 0, L - 1).astype(jnp.int32),
        "obs_count": draw_obs_count(jax.random.fold_in(jax.random.fold_in(key_of[11], part), 71), part),
        "reach": draw_reach(jax.random.fold_in(jax.random.fold_in(key_of[11], part), 71), part),
        "length_x": jnp.clip(jnp.exp(jax.random.uniform(key_of[6], (L,), jnp.float32, math.log(0.5), math.log(2.0))), 0.5, 2.0),
        "length_y": jnp.clip(jnp.exp(jax.random.uniform(key_of[7], (L,), jnp.float32, math.log(0.1), math.log(0.5))), 0.1, 0.5),
        "tilt": jnp.clip(jax.random.uniform(key_of[8], (L,), jnp.float32, -0.7, 0.7), -0.7, 0.7),
        "vert_len": jnp.clip(jnp.exp(jax.random.uniform(key_of[9], (L,), jnp.float32, math.log(1.5), math.log(12.0))), 1.5, 12.0),
        "balance": scatter_about(key_of[10], (L, L), L ** -0.5, 0.75, (), jnp.float32),
    }


def cover_tile(offset, fraction, cell_index, level_index, length_x, length_y, tilt, vert_len):
    column = jnp.arange(G_DEV, dtype=jnp.int32)
    grid_x = ((column // GY).astype(jnp.float32) + 0.5) / GX
    grid_y = ((column % GY).astype(jnp.float32) + 0.5) / GY
    obs_x = ((cell_index // GY).astype(jnp.float32) + fraction[0].astype(jnp.float32)) / GX
    obs_y = ((cell_index % GY).astype(jnp.float32) + fraction[1].astype(jnp.float32)) / GY
    east_gap = offset + grid_x[:, None] - obs_x[None, :]
    north_gap = grid_y[:, None] - obs_y[None, :]
    scaled_u = east_gap[None] / length_x[:, None, None]
    scaled_v = north_gap[None] / length_y[:, None, None]
    quadratic = scaled_u * scaled_u + scaled_v * scaled_v + 2.0 * tilt[:, None, None] * scaled_u * scaled_v
    horizontal = 1.0 / ((1.0 + quadratic) * (1.0 + quadratic))
    heights = jnp.arange(L, dtype=jnp.int32).astype(jnp.float32)
    separation = (heights[:, None] - level_index.astype(jnp.float32)[None, :]) / vert_len[:, None]
    vertical = 1.0 / (1.0 + separation * separation)
    return (horizontal * vertical[:, None, :]).astype(jnp.bfloat16)


def reference(obs_weight, obs_frac, obs_cell, obs_level, obs_count, reach, length_x, length_y, tilt, vert_len, balance):
    row_number = jnp.arange(OBS_DEV, dtype=jnp.int32)
    live = row_number[None, None, :] < obs_count[:, :, None]
    live_weight = jnp.where(live[..., None], obs_weight, jnp.zeros_like(obs_weight))

    def one_block(grid_block):
        running = jnp.zeros((L, G_DEV, C), jnp.float32)
        for offset in range(-REACH, REACH + 1):
            source = ((grid_block - offset) % BLOCKS).astype(jnp.int32)
            used = (offset <= reach[source, 1]) & (-offset <= reach[source, 0])
            for section in range(SECTIONS):
                tile = cover_tile(float(offset), obs_frac[source, section], obs_cell[source, section],
                                  obs_level[source, section], length_x, length_y, tilt, vert_len)
                term = jnp.einsum("lgo,oc->lgc", tile.astype(jnp.float32),
                                  live_weight[source, section].astype(jnp.float32),
                                  precision=lax.Precision.HIGHEST)
                running = running + jnp.where(used, term, jnp.zeros_like(term))
        return running

    analysis = lax.map(one_block, jnp.arange(BLOCKS, dtype=jnp.int32))
    analysis = jnp.transpose(analysis, (1, 0, 2, 3)).reshape(L, BLOCKS * G_DEV * C)
    increment = jnp.dot(balance, analysis, precision=lax.Precision.HIGHEST, preferred_element_type=jnp.float32)
    return increment.reshape(L, BLOCKS * G_DEV, C)
```

```python
import functools

import jax
import jax.numpy as jnp
from jax import lax
from jax.experimental import pallas as pl
from jax.experimental.pallas import tpu as pltpu
from jax.sharding import PartitionSpec as P

GX = 8
GY = 16
REACH = 3
TILE = 128
META = 8
MESH = pl.DeviceIdType.MESH


def gather_kernel(blocks, w_ref, frac_ref, cell_ref, level_ref, count_ref, reach_ref,
                  wo_ref, mo_ref, meta, w_send, w_recv, m_send, m_recv,
                  sw_send, sw_recv, sm_send, sm_recv, own_sem):
    blk = lax.axis_index("blk")
    sect = lax.axis_index("sect")
    sibling = 1 - sect
    offsets = [k for d in range(1, REACH + 1) for k in (d, -d)]

    barrier = pltpu.get_barrier_semaphore()
    for k in offsets:
        pl.semaphore_signal(barrier, inc=1, device_id={"blk": lax.rem(blk + k + blocks, blocks)},
                            device_id_type=MESH)
    pl.semaphore_signal(barrier, inc=1, device_id={"sect": sibling}, device_id_type=MESH)

    cell = cell_ref[...]
    frac = frac_ref[...].astype(jnp.float32)
    ox = ((cell // GY).astype(jnp.float32) + frac[0:1]) / GX
    oy = ((cell % GY).astype(jnp.float32) + frac[1:2]) / GY
    meta[0:1, :] = ox
    meta[1:2, :] = oy
    meta[2:3, :] = level_ref[...].astype(jnp.float32)
    wide = ox.shape
    meta[3:4, :] = jnp.broadcast_to(count_ref[...].astype(jnp.float32), wide)
    reach = reach_ref[...].astype(jnp.float32)
    meta[4:5, :] = jnp.broadcast_to(reach[:, 0:1], wide)
    meta[5:6, :] = jnp.broadcast_to(reach[:, 1:2], wide)
    meta[6:8, :] = jnp.zeros((2, wide[1]), jnp.float32)

    pl.semaphore_wait(barrier, len(offsets) + 1)

    copies = []
    for n, k in enumerate(offsets):
        target = {"blk": lax.rem(blk + k + blocks, blocks)}
        mc = pltpu.make_async_remote_copy(
            src_ref=meta, dst_ref=mo_ref.at[k + REACH, sect], send_sem=m_send.at[n],
            recv_sem=m_recv.at[n], device_id=target, device_id_type=MESH)
        wc = pltpu.make_async_remote_copy(
            src_ref=w_ref, dst_ref=wo_ref.at[k + REACH, sect], send_sem=w_send.at[n],
            recv_sem=w_recv.at[n], device_id=target, device_id_type=MESH)
        mc.start()
        wc.start()
        copies.append((k, mc, wc))

    last = len(offsets)
    passed = []

    def hand_over(n, k, w_from, m_from):
        mc = pltpu.make_async_remote_copy(
            src_ref=m_from, dst_ref=mo_ref.at[k + REACH, sect], send_sem=sm_send.at[n],
            recv_sem=sm_recv.at[n], device_id={"sect": sibling}, device_id_type=MESH)
        wc = pltpu.make_async_remote_copy(
            src_ref=w_from, dst_ref=wo_ref.at[k + REACH, sect], send_sem=sw_send.at[n],
            recv_sem=sw_recv.at[n], device_id={"sect": sibling}, device_id_type=MESH)
        mc.start()
        wc.start()
        passed.append((mc, wc))

    hand_over(last, 0, w_ref, meta)
    own_w = pltpu.make_async_copy(w_ref, wo_ref.at[REACH, sect], own_sem.at[0])
    own_m = pltpu.make_async_copy(meta, mo_ref.at[REACH, sect], own_sem.at[1])
    own_w.start()
    own_m.start()
    for n, (k, mc, wc) in enumerate(copies):
        mc.wait_recv()
        wc.wait_recv()
        hand_over(n, k, wo_ref.at[k + REACH, sect], mo_ref.at[k + REACH, sect])
    own_w.wait()
    own_m.wait()
    for k, mc, wc in copies:
        mc.wait_send()
        wc.wait_send()
    for mc, wc in passed:
        mc.wait()
        wc.wait()


def gather(blocks, weight, frac, cell, level, count, reach):
    rows, columns = weight.shape
    slots = 2 * REACH + 1
    sems = [pltpu.SemaphoreType.DMA((slots,)) for _ in range(8)]
    vmem = pl.BlockSpec(memory_space=pltpu.VMEM)
    hbm = pl.BlockSpec(memory_space=pl.ANY)
    return pl.pallas_call(
        functools.partial(gather_kernel, blocks),
        out_shape=(jax.ShapeDtypeStruct((slots, 2, rows, columns), weight.dtype),
                   jax.ShapeDtypeStruct((slots, 2, META, rows), jnp.float32)),
        in_specs=[hbm, vmem, vmem, vmem, vmem, vmem],
        out_specs=(hbm, hbm),
        scratch_shapes=[pltpu.VMEM((META, rows), jnp.float32)] + sems
        + [pltpu.SemaphoreType.DMA((2,))],
        compiler_params=pltpu.CompilerParams(collective_id=0, has_side_effects=True),
        name="gather_packets",
    )(weight, frac, cell, level, count, reach)


def spread_kernel(levels, half_x, sect_ref, w_ref, m_ref, m_hbm, lx_ref, ly_ref, tilt_ref,
                  vl_ref, bal_ref, out_ref, acc, info, picks, limits, wbuf, tabs, qtab, sem):
    slots, sections, rows = w_ref.shape[0], w_ref.shape[1], w_ref.shape[2]
    columns = w_ref.shape[3]
    half = half_x * GY
    fetch = pltpu.make_async_copy(m_hbm.at[:, :, :, pl.ds(0, TILE)], info, sem)
    fetch.start()

    eye = (lax.broadcasted_iota(jnp.int32, (levels, levels), 0)
           == lax.broadcasted_iota(jnp.int32, (levels, levels), 1))

    def column(ref):
        wide = jnp.broadcast_to(ref[...], (levels, levels))
        return jnp.sum(jnp.where(eye, wide, 0.0), axis=1, keepdims=True)

    lx, ly, tilt, vl = column(lx_ref), column(ly_ref), column(tilt_ref), column(vl_ref)
    wide = (levels, TILE)
    ratio = lx / ly
    tabs[0] = jnp.broadcast_to(tilt * ratio, wide)
    tabs[1] = jnp.broadcast_to((1.0 - tilt * tilt) * ratio * ratio, wide)
    tabs[2] = jnp.broadcast_to(lx * lx, wide)
    tabs[3] = jnp.broadcast_to(1.0 / vl, wide)
    ilx2 = 1.0 / (lx * lx)
    tabs[4] = jnp.broadcast_to(ilx2 * ilx2, wide)

    acc[...] = jnp.zeros_like(acc)
    fetch.wait()

    total = jnp.int32(0)
    for slot in range(slots):
        k = slot - REACH
        for s in range(sections):
            count = info[slot, s, 3, 0].astype(jnp.int32)
            low = info[slot, s, 4, 0].astype(jnp.int32)
            high = info[slot, s, 5, 0].astype(jnp.int32)
            inside = (k <= high) & (-k <= low)
            count = jnp.where(inside, count, 0)
            tiles = (count + TILE - 1) // TILE

            def put(t, at, count=count, slot=slot, s=s):
                picks[at] = (slot * sections + s) * (rows // TILE) + t
                limits[at] = count - t * TILE
                return at + 1

            total = lax.fori_loop(0, tiles, put, total)
    picks[total] = REACH * sections * (rows // TILE)
    limits[total] = 0

    x0 = sect_ref[0].astype(jnp.float32) * (half_x / GX)
    row = lax.broadcasted_iota(jnp.int32, (TILE, columns), 0)
    gy = (lax.broadcasted_iota(jnp.int32, (GY, TILE), 0).astype(jnp.float32) + 0.5) / GY
    heights = lax.broadcasted_iota(jnp.int32, wide, 0).astype(jnp.float32)
    group = 4

    def pair(step, carry):
        xs, ys = [], []
        for h in range(2):
            code = picks[2 * step + h]
            limit = limits[2 * step + h]
            t = lax.rem(code, rows // TILE)
            at = lax.div(code, rows // TILE)
            s = lax.rem(at, sections)
            slot = lax.div(at, sections)
            first = pl.multiple_of(t * TILE, TILE)
            w = w_ref[slot, s, pl.ds(first, TILE), :]
            wbuf[h * TILE:(h + 1) * TILE, :] = jnp.where(
                row < limit, w.astype(jnp.float32), 0.0).astype(w.dtype)
            lanes = pl.ds(first, TILE)
            ox = m_ref[slot, s, 0:1, lanes]
            oy = m_ref[slot, s, 1:2, lanes]
            lev = m_ref[slot, s, 2:3, lanes]
            offset = (slot - REACH).astype(jnp.float32) + x0
            xs.append([offset + (i + 0.5) / GX - ox for i in range(half_x)])
            ys.append(gy - oy)
            sep = (heights - lev) * tabs[3]
            qtab[h] = (1.0 + sep * sep) * tabs[4]
        y2s = [y * y for y in ys]
        xs = [[jnp.broadcast_to(x, (GY, TILE)) for x in line] for line in xs]

        def some(n, c):
            base = pl.multiple_of(n * 8, 8)
            for part in range(8 // group):
                halves = []
                for h in range(2):
                    pieces = []
                    for r in range(part * group, (part + 1) * group):
                        tv = tabs[0, pl.ds(base + r, 1), :]
                        td = tabs[1, pl.ds(base + r, 1), :]
                        t0 = tabs[2, pl.ds(base + r, 1), :]
                        q = qtab[h, pl.ds(base + r, 1), :]
                        v = ys[h] * tv
                        d = y2s[h] * td + t0
                        for i in range(half_x):
                            w = xs[h][i] + v
                            z = w * w + d
                            pieces.append(pl.reciprocal(z * z * q, approx=True)
                                          .astype(jnp.bfloat16))
                    halves.append(jnp.concatenate(pieces, axis=0))
                cover = jnp.concatenate(halves, axis=1)
                at = pl.ds(pl.multiple_of((base + part * group) * half, group * half), group * half)
                acc[at, :] += jnp.dot(cover, wbuf[...], preferred_element_type=jnp.float32)
            return c

        lax.fori_loop(0, levels // 8, some, 0)
        return carry

    lax.fori_loop(0, (total + 1) // 2, pair, 0)

    bal = bal_ref[...]
    bal_hi = bal.astype(jnp.bfloat16)
    bal_lo = (bal - bal_hi.astype(jnp.float32)).astype(jnp.bfloat16)
    left = jnp.concatenate([bal_hi, bal_hi, bal_lo], axis=1)

    def balance(n, c):
        g = n * 2
        a = jnp.concatenate([acc[pl.ds(g + e, levels, stride=half), :] for e in range(2)], axis=1)
        hi = a.astype(jnp.bfloat16)
        lo = (a - hi.astype(jnp.float32)).astype(jnp.bfloat16)
        right = jnp.concatenate([hi, lo, hi], axis=0)
        inc = jnp.dot(left, right, preferred_element_type=jnp.float32)
        for e in range(2):
            out_ref[pl.ds(g + e, levels, stride=half), :] = inc[:, e * columns:(e + 1) * columns]
        return c

    lax.fori_loop(0, half // 2, balance, 0)


def spread(sect, weights, metas, length_x, length_y, tilt, vert_len, balance):
    slots, sections, rows, columns = weights.shape
    levels = balance.shape[0]
    half_x = GX // sections
    half = half_x * GY
    tiles = slots * sections * (rows // TILE)
    vmem = pl.BlockSpec(memory_space=pltpu.VMEM)
    return pl.pallas_call(
        functools.partial(spread_kernel, levels, half_x),
        out_shape=jax.ShapeDtypeStruct((levels * half, columns), jnp.float32),
        in_specs=[pl.BlockSpec(memory_space=pltpu.SMEM), vmem, vmem,
                  pl.BlockSpec(memory_space=pl.ANY)] + [vmem] * 5,
        out_specs=vmem,
        scratch_shapes=[
            pltpu.VMEM((levels * half, columns), jnp.float32),
            pltpu.SMEM((slots, sections, META, TILE), jnp.float32),
            pltpu.SMEM((tiles + 2,), jnp.int32),
            pltpu.SMEM((tiles + 2,), jnp.int32),
            pltpu.VMEM((2 * TILE, columns), jnp.bfloat16),
            pltpu.VMEM((5, levels, TILE), jnp.float32),
            pltpu.VMEM((2, levels, TILE), jnp.float32),
            pltpu.SemaphoreType.DMA,
        ],
        compiler_params=pltpu.CompilerParams(vmem_limit_bytes=32 * 1024 * 1024),
        name="spread_and_balance",
    )(sect, weights, metas, metas, length_x, length_y, tilt, vert_len, balance)


def shards(blocks, obs_weight, obs_frac, obs_cell, obs_level, obs_count, reach,
           length_x, length_y, tilt, vert_len, balance):
    levels = balance.shape[0]
    columns = obs_weight.shape[3]
    sections = lax.axis_size("sect")
    weights, metas = gather(blocks, obs_weight[0, 0], obs_frac[0, 0], obs_cell[0], obs_level[0],
                            obs_count, reach)
    sect = lax.axis_index("sect")
    mixed = spread(sect.reshape(1).astype(jnp.int32), weights, metas, length_x[None],
                   length_y[None], tilt[None], vert_len[None], balance)
    half = mixed.shape[0] // levels
    mixed = mixed.reshape(sections, levels // sections, half, columns)
    mine = lax.dynamic_index_in_dim(mixed, sect, 0, keepdims=False)
    other = lax.dynamic_index_in_dim(mixed, 1 - sect, 0, keepdims=False)
    came = lax.ppermute(other, "sect", [(0, 1), (1, 0)])
    first = jnp.where(sect == 0, mine, came)
    second = jnp.where(sect == 0, came, mine)
    return jnp.concatenate([first, second], axis=1)


def solution(mesh):
    placed = (
        P(("date", "blk"), "sect", None, None),
        P(("date", "blk"), "sect", None, None),
        P(("date", "blk"), "sect", None),
        P(("date", "blk"), "sect", None),
        P(("date", "blk"), "sect"),
        P(("date", "blk"), None),
        P(),
        P(),
        P(),
        P(),
        P(),
    )
    return jax.shard_map(
        functools.partial(shards, mesh.shape["blk"]),
        mesh=mesh,
        in_specs=placed,
        out_specs=P("sect", ("date", "blk"), None),
        check_vma=False,
    )
```

```python
import functools

import jax
import jax.numpy as jnp
from jax import lax
from jax.experimental import pallas as pl
from jax.experimental.pallas import tpu as pltpu
from jax.sharding import PartitionSpec as P

GX = 8
GY = 16
REACH = 3
TILE = 128
META = 8
MESH = pl.DeviceIdType.MESH


def gather_kernel(blocks, w_ref, frac_ref, cell_ref, level_ref, count_ref, reach_ref,
                  wo_ref, mo_ref, meta, w_send, w_recv, m_send, m_recv,
                  sw_send, sw_recv, sm_send, sm_recv, own_sem):
    blk = lax.axis_index("blk")
    sect = lax.axis_index("sect")
    sibling = 1 - sect
    offsets = [k for d in range(1, REACH + 1) for k in (d, -d)]

    barrier = pltpu.get_barrier_semaphore()
    for k in offsets:
        pl.semaphore_signal(barrier, inc=1, device_id={"blk": lax.rem(blk + k + blocks, blocks)},
                            device_id_type=MESH)
    pl.semaphore_signal(barrier, inc=1, device_id={"sect": sibling}, device_id_type=MESH)

    cell = cell_ref[...]
    frac = frac_ref[...].astype(jnp.float32)
    ox = ((cell // GY).astype(jnp.float32) + frac[0:1]) / GX
    oy = ((cell % GY).astype(jnp.float32) + frac[1:2]) / GY
    meta[0:1, :] = ox
    meta[1:2, :] = oy
    meta[2:3, :] = level_ref[...].astype(jnp.float32)
    wide = ox.shape
    meta[3:4, :] = jnp.broadcast_to(count_ref[...].astype(jnp.float32), wide)
    reach = reach_ref[...].astype(jnp.float32)
    meta[4:5, :] = jnp.broadcast_to(reach[:, 0:1], wide)
    meta[5:6, :] = jnp.broadcast_to(reach[:, 1:2], wide)
    meta[6:8, :] = jnp.zeros((2, wide[1]), jnp.float32)

    pl.semaphore_wait(barrier, len(offsets) + 1)

    copies = []
    for n, k in enumerate(offsets):
        target = {"blk": lax.rem(blk + k + blocks, blocks)}
        mc = pltpu.make_async_remote_copy(
            src_ref=meta, dst_ref=mo_ref.at[k + REACH, sect], send_sem=m_send.at[n],
            recv_sem=m_recv.at[n], device_id=target, device_id_type=MESH)
        wc = pltpu.make_async_remote_copy(
            src_ref=w_ref, dst_ref=wo_ref.at[k + REACH, sect], send_sem=w_send.at[n],
            recv_sem=w_recv.at[n], device_id=target, device_id_type=MESH)
        mc.start()
        wc.start()
        copies.append((k, mc, wc))

    last = len(offsets)
    passed = []

    def hand_over(n, k, w_from, m_from):
        mc = pltpu.make_async_remote_copy(
            src_ref=m_from, dst_ref=mo_ref.at[k + REACH, sect], send_sem=sm_send.at[n],
            recv_sem=sm_recv.at[n], device_id={"sect": sibling}, device_id_type=MESH)
        wc = pltpu.make_async_remote_copy(
            src_ref=w_from, dst_ref=wo_ref.at[k + REACH, sect], send_sem=sw_send.at[n],
            recv_sem=sw_recv.at[n], device_id={"sect": sibling}, device_id_type=MESH)
        mc.start()
        wc.start()
        passed.append((mc, wc))

    hand_over(last, 0, w_ref, meta)
    own_w = pltpu.make_async_copy(w_ref, wo_ref.at[REACH, sect], own_sem.at[0])
    own_m = pltpu.make_async_copy(meta, mo_ref.at[REACH, sect], own_sem.at[1])
    own_w.start()
    own_m.start()
    for n, (k, mc, wc) in enumerate(copies):
        mc.wait_recv()
        wc.wait_recv()
        hand_over(n, k, wo_ref.at[k + REACH, sect], mo_ref.at[k + REACH, sect])
    own_w.wait()
    own_m.wait()
    for k, mc, wc in copies:
        mc.wait_send()
        wc.wait_send()
    for mc, wc in passed:
        mc.wait()
        wc.wait()


def gather(blocks, weight, frac, cell, level, count, reach):
    rows, columns = weight.shape
    slots = 2 * REACH + 1
    sems = [pltpu.SemaphoreType.DMA((slots,)) for _ in range(8)]
    vmem = pl.BlockSpec(memory_space=pltpu.VMEM)
    hbm = pl.BlockSpec(memory_space=pl.ANY)
    return pl.pallas_call(
        functools.partial(gather_kernel, blocks),
        out_shape=(jax.ShapeDtypeStruct((slots, 2, rows, columns), weight.dtype),
                   jax.ShapeDtypeStruct((slots, 2, META, rows), jnp.float32)),
        in_specs=[hbm, vmem, vmem, vmem, vmem, vmem],
        out_specs=(hbm, hbm),
        scratch_shapes=[pltpu.VMEM((META, rows), jnp.float32)] + sems
        + [pltpu.SemaphoreType.DMA((2,))],
        compiler_params=pltpu.CompilerParams(collective_id=0, has_side_effects=True),
        name="gather_packets",
    )(weight, frac, cell, level, count, reach)


def spread_kernel(levels, half_x, sect_ref, w_hbm, m_hbm, lx_hbm, ly_hbm, tilt_hbm, vl_hbm,
                  bal_hbm, mine_ref, other_ref, acc, w_all, m_all, info, lx_ref, ly_ref, tilt_ref,
                  vl_ref, bal_ref, live_w, live_m, cover, tabs, qtab, sems):
    sources, rows, columns = w_all.shape
    half = half_x * GY
    group = 8
    chunk = cover.shape[2]
    parts = chunk // TILE
    wanted = [(m_hbm.at[:, :, pl.ds(0, TILE)], info), (lx_hbm, lx_ref), (ly_hbm, ly_ref),
              (tilt_hbm, tilt_ref), (vl_hbm, vl_ref), (bal_hbm, bal_ref), (m_hbm, m_all),
              (w_hbm, w_all)]
    fetches = [pltpu.make_async_copy(src, dst, sems.at[n]) for n, (src, dst) in enumerate(wanted)]
    for fetch in fetches:
        fetch.start()
    acc[...] = jnp.zeros_like(acc)
    live_m[...] = jnp.zeros_like(live_m)
    cover[1] = jnp.zeros(cover.shape[1:], cover.dtype)
    for fetch in fetches[:6]:
        fetch.wait()

    eye = (lax.broadcasted_iota(jnp.int32, (levels, levels), 0)
           == lax.broadcasted_iota(jnp.int32, (levels, levels), 1))

    def column(ref):
        wide = jnp.broadcast_to(ref[...], (levels, levels))
        return jnp.sum(jnp.where(eye, wide, 0.0), axis=1, keepdims=True)

    lx, ly, tilt, vl = column(lx_ref), column(ly_ref), column(tilt_ref), column(vl_ref)
    ratio = lx / ly
    ilx2 = 1.0 / (lx * lx)
    entries = [tilt * ratio, (1.0 - tilt * tilt) * ratio * ratio, lx * lx]
    for n, entry in enumerate(entries):
        tabs[n] = jnp.broadcast_to(entry[:, :, None], (levels, 8, TILE))
    qtab[0] = jnp.broadcast_to(1.0 / vl, (levels, TILE))
    qtab[1] = jnp.broadcast_to(ilx2 * ilx2, (levels, TILE))

    for fetch in fetches[6:]:
        fetch.wait()
    x0 = sect_ref[0].astype(jnp.float32) * (half_x / GX) + 0.5 / GX
    row = lax.broadcasted_iota(jnp.int32, (TILE, columns), 0)
    lane = lax.broadcasted_iota(jnp.int32, (META, TILE), 1)
    field = lax.broadcasted_iota(jnp.int32, (META, TILE), 0)

    def pack(source, start):
        k = lax.div(source, sources // (2 * REACH + 1)) - REACH
        count = info[source, 3, 0].astype(jnp.int32)
        low = info[source, 4, 0].astype(jnp.int32)
        high = info[source, 5, 0].astype(jnp.int32)
        count = jnp.where((k <= high) & (-k <= low), count, 0)
        shift = lax.rem(start, TILE)
        base = k.astype(jnp.float32) + x0

        def put(t, c):
            first = pl.multiple_of(t * TILE, TILE)
            w = w_all[source, pl.ds(first, TILE), :]
            at = pl.ds(pl.multiple_of(start + first, 16), TILE)
            live_w[at, :] = jnp.where(row < count - first, w.astype(jnp.float32),
                                      0.0).astype(w.dtype)
            m = m_all[source, :, pl.ds(first, TILE)]
            m = pltpu.roll(jnp.where(field == 0, base - m, m), shift, 1)
            here = lax.div(start, TILE) + t
            live_m[here] = jnp.where(lane >= shift, m, live_m[here])
            live_m[here + 1] = jnp.where(lane < shift, m, live_m[here + 1])
            return c

        lax.fori_loop(0, (count + TILE - 1) // TILE, put, 0)
        return start + ((count + 15) // 16) * 16

    total = lax.fori_loop(0, sources, pack, jnp.int32(0))
    live_w[pl.ds(pl.multiple_of(total, 16), chunk), :] = jnp.zeros((chunk, columns), live_w.dtype)
    chunks = (total + chunk - 1) // chunk

    gy = [(lax.broadcasted_iota(jnp.int32, (8, TILE), 0).astype(jnp.float32) + (8 * e + 0.5)) / GY
          for e in range(GY // 8)]
    rises = lax.broadcasted_iota(jnp.int32, (group, TILE), 0)

    def make(slot, block, first_level):
        heights = (rises + first_level).astype(jnp.float32)
        ivl = qtab[0, pl.ds(first_level, group), :]
        scale = qtab[1, pl.ds(first_level, group), :]
        for h in range(parts):
            m = live_m[block * parts + h]
            sep = (heights - m[2:3]) * ivl
            qs = (1.0 + sep * sep) * scale
            xs = [jnp.broadcast_to(m[0:1] + i / GX, (8, TILE)) for i in range(half_x)]
            ys = [g - m[1:2] for g in gy]
            y2s = [y * y for y in ys]
            for r in range(group):
                tv = tabs[0, first_level + r]
                td = tabs[1, first_level + r]
                t0 = tabs[2, first_level + r]
                q = jnp.broadcast_to(qs[r:r + 1], (8, TILE))
                vs = [y * tv for y in ys]
                ds = [y2 * td + t0 for y2 in y2s]
                for i in range(half_x):
                    done = []
                    for v, d in zip(vs, ds):
                        w = xs[i] + v
                        z = w * w + d
                        done.append(pl.reciprocal(z * z * q, approx=True))
                    at = r * half + i * GY
                    cover[slot, at:at + GY, h * TILE:(h + 1) * TILE] = jnp.concatenate(
                        done, axis=0).astype(jnp.bfloat16)

    def use(slot, block, first_level):
        w = live_w[pl.ds(pl.multiple_of(block * chunk, chunk), chunk), :]
        at = pl.ds(pl.multiple_of(first_level * half, group * half), group * half)
        acc[at, :] += jnp.dot(cover[slot], w, preferred_element_type=jnp.float32)

    turns = levels // (2 * group)

    def turn(step, c):
        block = lax.div(step, turns)
        level = pl.multiple_of(lax.rem(step, turns) * (2 * group), 2 * group)
        before = jnp.maximum(step - 1, 0)
        use(1, lax.div(before, turns), lax.rem(before, turns) * (2 * group) + group)
        make(0, block, level)
        use(0, block, level)
        make(1, block, level + group)
        return c

    lax.fori_loop(0, chunks * turns, turn, 0)
    use(1, chunks - 1, levels - group)

    share = levels // 2
    sect = sect_ref[0]
    bal = jnp.concatenate([bal_ref[pl.ds(pl.multiple_of(sect * share, share), share), :],
                           bal_ref[pl.ds(pl.multiple_of((1 - sect) * share, share), share), :]],
                          axis=0)
    bal_hi = bal.astype(jnp.bfloat16)
    bal_lo = (bal - bal_hi.astype(jnp.float32)).astype(jnp.bfloat16)
    left = jnp.concatenate([bal_hi, bal_hi, bal_lo], axis=1)

    def balance(n, c):
        for m in range(4):
            g = n * 8 + m * 2
            a = jnp.concatenate([acc[pl.ds(g + e, levels, stride=half), :] for e in range(2)],
                                axis=1)
            hi = a.astype(jnp.bfloat16)
            lo = (a - hi.astype(jnp.float32)).astype(jnp.bfloat16)
            right = jnp.concatenate([hi, lo, hi], axis=0)
            inc = jnp.dot(left, right, preferred_element_type=jnp.float32)
            for e in range(2):
                at = pl.ds(g + e, share, stride=half)
                mine_ref[at, :] = inc[:share, e * columns:(e + 1) * columns]
                other_ref[at, :] = inc[share:, e * columns:(e + 1) * columns]
        return c

    lax.fori_loop(0, half // 8, balance, 0)


def spread(sect, weights, metas, length_x, length_y, tilt, vert_len, balance):
    slots, sections, rows, columns = weights.shape
    sources = slots * sections
    weights = weights.reshape(sources, rows, columns)
    metas = metas.reshape(sources, META, rows)
    levels = balance.shape[0]
    half_x = GX // sections
    half = half_x * GY
    chunk = 4 * TILE
    live = sources * rows + chunk
    vmem = pl.BlockSpec(memory_space=pltpu.VMEM)
    hbm = pl.BlockSpec(memory_space=pltpu.HBM)
    out = jax.ShapeDtypeStruct((levels // 2 * half, columns), jnp.float32)
    line = pltpu.VMEM((1, levels), jnp.float32)
    return pl.pallas_call(
        functools.partial(spread_kernel, levels, half_x),
        out_shape=(out, out),
        in_specs=[pl.BlockSpec(memory_space=pltpu.SMEM)] + [hbm] * 7,
        out_specs=(vmem, vmem),
        scratch_shapes=[
            pltpu.VMEM((levels * half, columns), jnp.float32),
            pltpu.VMEM((sources, rows, columns), jnp.bfloat16),
            pltpu.VMEM((sources, META, rows), jnp.float32),
            pltpu.SMEM((sources, META, TILE), jnp.float32),
            line, line, line, line,
            pltpu.VMEM((levels, levels), jnp.float32),
            pltpu.VMEM((live, columns), jnp.bfloat16),
            pltpu.VMEM((live // TILE + 1, META, TILE), jnp.float32),
            pltpu.VMEM((2, 8 * half, chunk), jnp.bfloat16),
            pltpu.VMEM((3, levels, 8, TILE), jnp.float32),
            pltpu.VMEM((2, levels, TILE), jnp.float32),
            pltpu.SemaphoreType.DMA((8,)),
        ],
        compiler_params=pltpu.CompilerParams(vmem_limit_bytes=32 * 1024 * 1024),
        name="spread_and_balance",
    )(sect, weights, metas, length_x, length_y, tilt, vert_len, balance)


def shards(blocks, obs_weight, obs_frac, obs_cell, obs_level, obs_count, reach,
           length_x, length_y, tilt, vert_len, balance):
    levels = balance.shape[0]
    columns = obs_weight.shape[3]
    sections = lax.axis_size("sect")
    weights, metas = gather(blocks, obs_weight[0, 0], obs_frac[0, 0], obs_cell[0], obs_level[0],
                            obs_count, reach)
    sect = lax.axis_index("sect")
    mine, other = spread(sect.reshape(1).astype(jnp.int32), weights, metas, length_x[None],
                         length_y[None], tilt[None], vert_len[None], balance)
    shape = (levels // sections, -1, columns)
    came = lax.ppermute(other.reshape(shape), "sect", [(0, 1), (1, 0)])
    mine = mine.reshape(shape)
    first = jnp.where(sect == 0, mine, came)
    second = jnp.where(sect == 0, came, mine)
    return jnp.concatenate([first, second], axis=1)


def solution(mesh):
    placed = (
        P(("date", "blk"), "sect", None, None),
        P(("date", "blk"), "sect", None, None),
        P(("date", "blk"), "sect", None),
        P(("date", "blk"), "sect", None),
        P(("date", "blk"), "sect"),
        P(("date", "blk"), None),
        P(),
        P(),
        P(),
        P(),
        P(),
    )
    return jax.shard_map(
        functools.partial(shards, mesh.shape["blk"]),
        mesh=mesh,
        in_specs=placed,
        out_specs=P("sect", ("date", "blk"), None),
        check_vma=False,
    )
```

```python
import functools

import jax
import jax.numpy as jnp
from jax import lax
from jax.experimental import pallas as pl
from jax.experimental.pallas import tpu as pltpu
from jax.sharding import PartitionSpec as P

GX = 8
GY = 16
REACH = 3
TILE = 128
META = 4
VMEM_BYTES = 60 * 1024 * 1024
MESH = pl.DeviceIdType.MESH


def gather_kernel(blocks, w_ref, frac_ref, cell_ref, level_ref, count_ref, reach_ref,
                  wo_ref, mo_ref, meta, d_send, d_recv, r_send, r_recv, s_send, s_recv, own_sem):
    blk = lax.axis_index("blk")
    sect = lax.axis_index("sect")
    sibling = {"sect": 1 - sect}
    toward = 1 - 2 * lax.rem(blk, 2)
    rows = w_ref.shape[0]
    cut = rows // 2

    def at(k):
        return {"blk": lax.rem(blk + k + blocks, blocks)}

    direct = [2, -2, toward, -3 * toward]
    origin = [2, -2, -toward, 3 * toward]
    barrier = pltpu.get_barrier_semaphore()
    for k in direct:
        pl.semaphore_signal(barrier, inc=1, device_id=at(k), device_id_type=MESH)
    pl.semaphore_signal(barrier, inc=1, device_id=sibling, device_id_type=MESH)

    cell = cell_ref[...]
    frac = frac_ref[...].astype(jnp.float32)
    meta[0:1, :] = ((cell // GY).astype(jnp.float32) + frac[0:1]) / GX
    meta[1:2, :] = ((cell % GY).astype(jnp.float32) + frac[1:2]) / GY
    meta[2:3, :] = level_ref[...].astype(jnp.float32)
    lane = lax.broadcasted_iota(jnp.int32, cell.shape, 1)
    reach = reach_ref[...].astype(jnp.float32)
    meta[3:4, :] = jnp.where(lane == 0, count_ref[...].astype(jnp.float32),
                             jnp.where(lane == 1, reach[:, 0:1], reach[:, 1:2]))

    pl.semaphore_wait(barrier, len(direct) + 1)

    def kept(k, part):
        if part == 0:
            return mo_ref.at[k + REACH, sect]
        return wo_ref.at[k + REACH, sect, pl.ds((part - 1) * cut, cut)]

    def mine(part):
        return meta if part == 0 else w_ref.at[pl.ds((part - 1) * cut, cut)]

    def copy(src, k, part, send, recv, n, target):
        return pltpu.make_async_remote_copy(
            src_ref=src, dst_ref=kept(k, part), send_sem=send.at[n, part],
            recv_sem=recv.at[n, part], device_id=target, device_id_type=MESH)

    sent = []

    def launch(*what):
        c = copy(*what)
        c.start()
        sent.append(c)

    def share(src, k, part, n):
        launch(src, k, part, s_send, s_recv, n, sibling)

    for part in range(3):
        for n in range(3):
            launch(mine(part), direct[n], part, d_send, d_recv, n, at(direct[n]))
    for part in range(3):
        share(mine(part), 0, part, 6)
    for part in range(3):
        launch(mine(part), direct[3], part, d_send, d_recv, 3, at(direct[3]))
    own = [pltpu.make_async_copy(mine(part), kept(0, part), own_sem.at[part]) for part in range(3)]
    for c in own:
        c.start()

    def arrive(k, part, recv, n):
        copy(kept(k, part), k, part, d_send, recv, n, sibling).wait_recv()

    for part in range(3):
        for n in range(2):
            k = origin[n]
            arrive(k, part, d_recv, n)
            launch(kept(k, part), toward + k, part, r_send, r_recv, n, at(toward))
            share(kept(k, part), k, part, n)
        arrive(origin[2], part, d_recv, 2)
        share(kept(origin[2], part), origin[2], part, 2)
    for part in range(3):
        arrive(origin[3], part, d_recv, 3)
        share(kept(origin[3], part), origin[3], part, 3)
        for n in range(2):
            k = origin[n] - toward
            arrive(k, part, r_recv, n)
            share(kept(k, part), k, part, 4 + n)
    for c in own:
        c.wait()
    for c in sent:
        c.wait_send()
    for n in range(7):
        for part in range(3):
            arrive(0, part, s_recv, n)


def gather(blocks, weight, frac, cell, level, count, reach):
    rows, columns = weight.shape
    slots = 2 * REACH + 1
    sems = [pltpu.SemaphoreType.DMA((n, 3)) for n in (4, 4, 2, 2, slots, slots)]
    vmem = pl.BlockSpec(memory_space=pltpu.VMEM)
    hbm = pl.BlockSpec(memory_space=pl.ANY)
    return pl.pallas_call(
        functools.partial(gather_kernel, blocks),
        out_shape=(jax.ShapeDtypeStruct((slots, 2, rows, columns), weight.dtype),
                   jax.ShapeDtypeStruct((slots, 2, META, rows), jnp.float32)),
        in_specs=[hbm, vmem, vmem, vmem, vmem, vmem],
        out_specs=(hbm, hbm),
        scratch_shapes=[pltpu.VMEM((META, rows), jnp.float32)] + sems
        + [pltpu.SemaphoreType.DMA((3,))],
        compiler_params=pltpu.CompilerParams(collective_id=0, has_side_effects=True),
        name="gather_packets",
    )(weight, frac, cell, level, count, reach)


def spread_kernel(levels, half_x, sect_ref, w_hbm, m_hbm, lx_hbm, ly_hbm, tilt_hbm, vl_hbm,
                  bal_hbm, mine_ref, other_ref, acc, w_all, m_all, info, lx_ref, ly_ref, tilt_ref,
                  vl_ref, bal_ref, live_w, live_m, cover, tabs, qtab, sems):
    sources, rows, columns = w_all.shape
    half = half_x * GY
    group = 8
    chunk = cover.shape[2]
    parts = chunk // TILE
    wanted = [(m_hbm.at[:, :, pl.ds(0, TILE)], info), (lx_hbm, lx_ref), (ly_hbm, ly_ref),
              (tilt_hbm, tilt_ref), (vl_hbm, vl_ref), (bal_hbm, bal_ref), (m_hbm, m_all),
              (w_hbm, w_all)]
    fetches = [pltpu.make_async_copy(src, dst, sems.at[n]) for n, (src, dst) in enumerate(wanted)]
    for fetch in fetches:
        fetch.start()
    acc[...] = jnp.zeros_like(acc)
    live_m[...] = jnp.zeros_like(live_m)
    cover[1] = jnp.zeros(cover.shape[1:], cover.dtype)
    for fetch in fetches[:6]:
        fetch.wait()

    eye = (lax.broadcasted_iota(jnp.int32, (levels, levels), 0)
           == lax.broadcasted_iota(jnp.int32, (levels, levels), 1))

    def column(ref):
        wide = jnp.broadcast_to(ref[...], (levels, levels))
        return jnp.sum(jnp.where(eye, wide, 0.0), axis=1, keepdims=True)

    lx, ly, tilt, vl = column(lx_ref), column(ly_ref), column(tilt_ref), column(vl_ref)
    ratio = lx / ly
    ilx2 = 1.0 / (lx * lx)
    entries = [tilt * ratio, (1.0 - tilt * tilt) * ratio * ratio, lx * lx]
    for n, entry in enumerate(entries):
        tabs[n] = jnp.broadcast_to(entry[:, :, None], (levels, 8, TILE))
    qtab[0] = jnp.broadcast_to(1.0 / vl, (levels, TILE))
    qtab[1] = jnp.broadcast_to(ilx2 * ilx2, (levels, TILE))

    for fetch in fetches[6:]:
        fetch.wait()
    x0 = sect_ref[0].astype(jnp.float32) * (half_x / GX) + 0.5 / GX
    row = lax.broadcasted_iota(jnp.int32, (TILE, columns), 0)
    lane = lax.broadcasted_iota(jnp.int32, (META, TILE), 1)
    field = lax.broadcasted_iota(jnp.int32, (META, TILE), 0)

    def pack(source, start):
        k = lax.div(source, sources // (2 * REACH + 1)) - REACH
        count = info[source, 3, 0].astype(jnp.int32)
        low = info[source, 3, 1].astype(jnp.int32)
        high = info[source, 3, 2].astype(jnp.int32)
        count = jnp.where((k <= high) & (-k <= low), count, 0)
        shift = lax.rem(start, TILE)
        base = k.astype(jnp.float32) + x0

        def put(t, c):
            first = pl.multiple_of(t * TILE, TILE)
            w = w_all[source, pl.ds(first, TILE), :]
            at = pl.ds(pl.multiple_of(start + first, 16), TILE)
            live_w[at, :] = jnp.where(row < count - first, w.astype(jnp.float32),
                                      0.0).astype(w.dtype)
            m = m_all[source, :, pl.ds(first, TILE)]
            m = pltpu.roll(jnp.where(field == 0, base - m, m), shift, 1)
            here = lax.div(start, TILE) + t
            live_m[here] = jnp.where(lane >= shift, m, live_m[here])
            live_m[here + 1] = jnp.where(lane < shift, m, live_m[here + 1])
            return c

        lax.fori_loop(0, (count + TILE - 1) // TILE, put, 0)
        return start + ((count + 15) // 16) * 16

    total = lax.fori_loop(0, sources, pack, jnp.int32(0))
    live_w[pl.ds(pl.multiple_of(total, 16), chunk), :] = jnp.zeros((chunk, columns), live_w.dtype)
    chunks = (total + chunk - 1) // chunk

    gy = [(lax.broadcasted_iota(jnp.int32, (8, TILE), 0).astype(jnp.float32) + (8 * e + 0.5)) / GY
          for e in range(GY // 8)]
    rises = lax.broadcasted_iota(jnp.int32, (group, TILE), 0)

    def make(slot, block, first_level):
        heights = (rises + first_level).astype(jnp.float32)
        ivl = qtab[0, pl.ds(first_level, group), :]
        scale = qtab[1, pl.ds(first_level, group), :]
        for h in range(parts):
            m = live_m[block * parts + h]
            sep = (heights - m[2:3]) * ivl
            qs = (1.0 + sep * sep) * scale
            xs = [jnp.broadcast_to(m[0:1] + i / GX, (8, TILE)) for i in range(half_x)]
            ys = [g - m[1:2] for g in gy]
            y2s = [y * y for y in ys]
            for r in range(group):
                tv = tabs[0, first_level + r]
                td = tabs[1, first_level + r]
                t0 = tabs[2, first_level + r]
                q = jnp.broadcast_to(qs[r:r + 1], (8, TILE))
                vs = [y * tv for y in ys]
                ds = [y2 * td + t0 for y2 in y2s]
                for i in range(half_x):
                    done = []
                    for v, d in zip(vs, ds):
                        w = xs[i] + v
                        z = w * w + d
                        done.append(z * z * q)
                    both = pl.reciprocal(done[0] * done[1], approx=True)
                    done = [both * done[1], both * done[0]]
                    at = r * half + i * GY
                    cover[slot, at:at + GY, h * TILE:(h + 1) * TILE] = jnp.concatenate(
                        done, axis=0).astype(jnp.bfloat16)

    def use(slot, block, first_level):
        w = live_w[pl.ds(pl.multiple_of(block * chunk, chunk), chunk), :]
        at = pl.ds(pl.multiple_of(first_level * half, group * half), group * half)
        acc[at, :] += jnp.dot(cover[slot], w, preferred_element_type=jnp.float32)

    turns = levels // (2 * group)

    def turn(step, c):
        block = lax.div(step, turns)
        level = pl.multiple_of(lax.rem(step, turns) * (2 * group), 2 * group)
        before = jnp.maximum(step - 1, 0)
        use(1, lax.div(before, turns), lax.rem(before, turns) * (2 * group) + group)
        make(0, block, level)
        use(0, block, level)
        make(1, block, level + group)
        return c

    lax.fori_loop(0, chunks * turns, turn, 0)
    use(1, chunks - 1, levels - group)

    share = levels // 2
    sect = sect_ref[0]
    bal = jnp.concatenate([bal_ref[pl.ds(pl.multiple_of(sect * share, share), share), :],
                           bal_ref[pl.ds(pl.multiple_of((1 - sect) * share, share), share), :]],
                          axis=0)
    bal_hi = bal.astype(jnp.bfloat16)
    bal_lo = (bal - bal_hi.astype(jnp.float32)).astype(jnp.bfloat16)
    left = jnp.concatenate([bal_hi, bal_hi, bal_lo], axis=1)

    def balance(n, c):
        for m in range(4):
            g = n * 8 + m * 2
            a = jnp.concatenate([acc[pl.ds(g + e, levels, stride=half), :] for e in range(2)],
                                axis=1)
            hi = a.astype(jnp.bfloat16)
            lo = (a - hi.astype(jnp.float32)).astype(jnp.bfloat16)
            right = jnp.concatenate([hi, lo, hi], axis=0)
            inc = jnp.dot(left, right, preferred_element_type=jnp.float32)
            for e in range(2):
                at = pl.ds(g + e, share, stride=half)
                mine_ref[at, :] = inc[:share, e * columns:(e + 1) * columns]
                other_ref[at, :] = inc[share:, e * columns:(e + 1) * columns]
        return c

    lax.fori_loop(0, half // 8, balance, 0)


def spread(sect, weights, metas, length_x, length_y, tilt, vert_len, balance):
    slots, sections, rows, columns = weights.shape
    sources = slots * sections
    weights = weights.reshape(sources, rows, columns)
    metas = metas.reshape(sources, META, rows)
    levels = balance.shape[0]
    half_x = GX // sections
    half = half_x * GY
    chunk = 4 * TILE
    live = sources * rows + chunk
    vmem = pl.BlockSpec(memory_space=pltpu.VMEM)
    hbm = pl.BlockSpec(memory_space=pltpu.HBM)
    out = jax.ShapeDtypeStruct((levels // 2 * half, columns), jnp.float32)
    line = pltpu.VMEM((1, levels), jnp.float32)
    return pl.pallas_call(
        functools.partial(spread_kernel, levels, half_x),
        out_shape=(out, out),
        in_specs=[pl.BlockSpec(memory_space=pltpu.SMEM)] + [hbm] * 7,
        out_specs=(vmem, vmem),
        scratch_shapes=[
            pltpu.VMEM((levels * half, columns), jnp.float32),
            pltpu.VMEM((sources, rows, columns), jnp.bfloat16),
            pltpu.VMEM((sources, META, rows), jnp.float32),
            pltpu.SMEM((sources, META, TILE), jnp.float32),
            line, line, line, line,
            pltpu.VMEM((levels, levels), jnp.float32),
            pltpu.VMEM((live, columns), jnp.bfloat16),
            pltpu.VMEM((live // TILE + 1, META, TILE), jnp.float32),
            pltpu.VMEM((2, 8 * half, chunk), jnp.bfloat16),
            pltpu.VMEM((3, levels, 8, TILE), jnp.float32),
            pltpu.VMEM((2, levels, TILE), jnp.float32),
            pltpu.SemaphoreType.DMA((8,)),
        ],
        compiler_params=pltpu.CompilerParams(vmem_limit_bytes=VMEM_BYTES),
        name="spread_and_balance",
    )(sect, weights, metas, length_x, length_y, tilt, vert_len, balance)


def shards(blocks, obs_weight, obs_frac, obs_cell, obs_level, obs_count, reach,
           length_x, length_y, tilt, vert_len, balance):
    levels = balance.shape[0]
    columns = obs_weight.shape[3]
    sections = lax.axis_size("sect")
    weights, metas = gather(blocks, obs_weight[0, 0], obs_frac[0, 0], obs_cell[0], obs_level[0],
                            obs_count, reach)
    sect = lax.axis_index("sect")
    mine, other = spread(sect.reshape(1).astype(jnp.int32), weights, metas, length_x[None],
                         length_y[None], tilt[None], vert_len[None], balance)
    shape = (levels // sections, -1, columns)
    came = lax.ppermute(other.reshape(shape), "sect", [(0, 1), (1, 0)])
    mine = mine.reshape(shape)
    first = jnp.where(sect == 0, mine, came)
    second = jnp.where(sect == 0, came, mine)
    return jnp.concatenate([first, second], axis=1)


def solution(mesh):
    placed = (
        P(("date", "blk"), "sect", None, None),
        P(("date", "blk"), "sect", None, None),
        P(("date", "blk"), "sect", None),
        P(("date", "blk"), "sect", None),
        P(("date", "blk"), "sect"),
        P(("date", "blk"), None),
        P(),
        P(),
        P(),
        P(),
        P(),
    )
    return jax.shard_map(
        functools.partial(shards, mesh.shape["blk"]),
        mesh=mesh,
        in_specs=placed,
        out_specs=P("sect", ("date", "blk"), None),
        check_vma=False,
    )
```

```python
import functools

import jax
import jax.numpy as jnp
from jax import lax
from jax.experimental import pallas as pl
from jax.experimental.pallas import tpu as pltpu
from jax.sharding import PartitionSpec as P

GX = 8
GY = 16
REACH = 3
TILE = 128
META = 4
VMEM_BYTES = 60 * 1024 * 1024
MESH = pl.DeviceIdType.MESH


def gather_kernel(blocks, w_ref, frac_ref, cell_ref, level_ref, count_ref, reach_ref,
                  wo_ref, mo_ref, meta, d_send, d_recv, r_send, r_recv, s_send, s_recv, own_sem):
    blk = lax.axis_index("blk")
    sect = lax.axis_index("sect")
    sibling = {"sect": 1 - sect}
    toward = 1 - 2 * lax.rem(blk, 2)
    rows = w_ref.shape[0]
    cut = rows // 2

    def at(k):
        return {"blk": lax.rem(blk + k + blocks, blocks)}

    direct = [2, -2, toward, -3 * toward]
    origin = [2, -2, -toward, 3 * toward]
    barrier = pltpu.get_barrier_semaphore()
    for k in direct:
        pl.semaphore_signal(barrier, inc=1, device_id=at(k), device_id_type=MESH)
    pl.semaphore_signal(barrier, inc=1, device_id=sibling, device_id_type=MESH)

    cell = cell_ref[...]
    frac = frac_ref[...].astype(jnp.float32)
    meta[0:1, :] = ((cell // GY).astype(jnp.float32) + frac[0:1]) / GX
    meta[1:2, :] = ((cell % GY).astype(jnp.float32) + frac[1:2]) / GY
    meta[2:3, :] = level_ref[...].astype(jnp.float32)
    lane = lax.broadcasted_iota(jnp.int32, cell.shape, 1)
    reach = reach_ref[...].astype(jnp.float32)
    meta[3:4, :] = jnp.where(lane == 0, count_ref[...].astype(jnp.float32),
                             jnp.where(lane == 1, reach[:, 0:1], reach[:, 1:2]))

    pl.semaphore_wait(barrier, len(direct) + 1)

    def kept(k, part):
        if part == 0:
            return mo_ref.at[k + REACH, sect]
        return wo_ref.at[k + REACH, sect, pl.ds((part - 1) * cut, cut)]

    def mine(part):
        return meta if part == 0 else w_ref.at[pl.ds((part - 1) * cut, cut)]

    def copy(src, k, part, send, recv, n, target):
        return pltpu.make_async_remote_copy(
            src_ref=src, dst_ref=kept(k, part), send_sem=send.at[n, part],
            recv_sem=recv.at[n, part], device_id=target, device_id_type=MESH)

    sent = []

    def launch(*what):
        c = copy(*what)
        c.start()
        sent.append(c)

    def share(src, k, part, n):
        launch(src, k, part, s_send, s_recv, n, sibling)

    for part in range(3):
        for n in range(3):
            launch(mine(part), direct[n], part, d_send, d_recv, n, at(direct[n]))
    for part in range(3):
        share(mine(part), 0, part, 6)
    for part in range(3):
        launch(mine(part), direct[3], part, d_send, d_recv, 3, at(direct[3]))
    own = [pltpu.make_async_copy(mine(part), kept(0, part), own_sem.at[part]) for part in range(3)]
    for c in own:
        c.start()

    def arrive(k, part, recv, n):
        copy(kept(k, part), k, part, d_send, recv, n, sibling).wait_recv()

    for part in range(3):
        for n in range(2):
            k = origin[n]
            arrive(k, part, d_recv, n)
            launch(kept(k, part), toward + k, part, r_send, r_recv, n, at(toward))
            share(kept(k, part), k, part, n)
        arrive(origin[2], part, d_recv, 2)
        share(kept(origin[2], part), origin[2], part, 2)
    for part in range(3):
        arrive(origin[3], part, d_recv, 3)
        share(kept(origin[3], part), origin[3], part, 3)
        for n in range(2):
            k = origin[n] - toward
            arrive(k, part, r_recv, n)
            share(kept(k, part), k, part, 4 + n)
    for c in own:
        c.wait()
    for c in sent:
        c.wait_send()
    for n in range(7):
        for part in range(3):
            arrive(0, part, s_recv, n)


def gather(blocks, weight, frac, cell, level, count, reach):
    rows, columns = weight.shape
    slots = 2 * REACH + 1
    sems = [pltpu.SemaphoreType.DMA((n, 3)) for n in (4, 4, 2, 2, slots, slots)]
    vmem = pl.BlockSpec(memory_space=pltpu.VMEM)
    hbm = pl.BlockSpec(memory_space=pl.ANY)
    return pl.pallas_call(
        functools.partial(gather_kernel, blocks),
        out_shape=(jax.ShapeDtypeStruct((slots, 2, rows, columns), weight.dtype),
                   jax.ShapeDtypeStruct((slots, 2, META, rows), jnp.float32)),
        in_specs=[hbm, vmem, vmem, vmem, vmem, vmem],
        out_specs=(hbm, hbm),
        scratch_shapes=[pltpu.VMEM((META, rows), jnp.float32)] + sems
        + [pltpu.SemaphoreType.DMA((3,))],
        compiler_params=pltpu.CompilerParams(collective_id=0, has_side_effects=True),
        name="gather_packets",
    )(weight, frac, cell, level, count, reach)


def spread_kernel(levels, half_x, sect_ref, w_hbm, m_hbm, lx_hbm, ly_hbm, tilt_hbm, vl_hbm,
                  bal_hbm, part_ref, other_ref, acc, mine, out_sem, w_all, m_all, info, lx_ref, ly_ref, tilt_ref,
                  vl_ref, bal_ref, live_w, live_m, cover, tabs, qtab, sems):
    sources, rows, columns = w_all.shape
    half = half_x * GY
    group = 8
    parts = cover.shape[1]
    chunk = parts * TILE
    wanted = [(m_hbm.at[:, :, pl.ds(0, TILE)], info), (lx_hbm, lx_ref), (ly_hbm, ly_ref),
              (tilt_hbm, tilt_ref), (vl_hbm, vl_ref), (bal_hbm, bal_ref), (m_hbm, m_all),
              (w_hbm, w_all)]
    fetches = [pltpu.make_async_copy(src, dst, sems.at[n]) for n, (src, dst) in enumerate(wanted)]
    for fetch in fetches:
        fetch.start()
    acc[...] = jnp.zeros_like(acc)
    live_m[...] = jnp.zeros_like(live_m)
    cover[1] = jnp.zeros(cover.shape[1:], cover.dtype)
    for fetch in fetches[:6]:
        fetch.wait()

    eye = (lax.broadcasted_iota(jnp.int32, (levels, levels), 0)
           == lax.broadcasted_iota(jnp.int32, (levels, levels), 1))

    def column(ref):
        wide = jnp.broadcast_to(ref[...], (levels, levels))
        return jnp.sum(jnp.where(eye, wide, 0.0), axis=1, keepdims=True)

    lx, ly, tilt, vl = column(lx_ref), column(ly_ref), column(tilt_ref), column(vl_ref)
    ratio = lx / ly
    ilx2 = 1.0 / (lx * lx)
    entries = [tilt * ratio, (1.0 - tilt * tilt) * ratio * ratio, lx * lx]
    for n, entry in enumerate(entries):
        tabs[n] = jnp.broadcast_to(entry[:, :, None], (levels, 8, TILE))
    qtab[0] = jnp.broadcast_to(1.0 / vl, (levels, TILE))
    qtab[1] = jnp.broadcast_to(ilx2 * ilx2, (levels, TILE))

    for fetch in fetches[6:]:
        fetch.wait()
    x0 = sect_ref[0].astype(jnp.float32) * (half_x / GX) + 0.5 / GX
    row = lax.broadcasted_iota(jnp.int32, (TILE, columns), 0)
    lane = lax.broadcasted_iota(jnp.int32, (META, TILE), 1)
    field = lax.broadcasted_iota(jnp.int32, (META, TILE), 0)

    def pack(source, start):
        k = lax.div(source, sources // (2 * REACH + 1)) - REACH
        count = info[source, 3, 0].astype(jnp.int32)
        low = info[source, 3, 1].astype(jnp.int32)
        high = info[source, 3, 2].astype(jnp.int32)
        count = jnp.where((k <= high) & (-k <= low), count, 0)
        shift = lax.rem(start, TILE)
        base = k.astype(jnp.float32) + x0

        def put(t, c):
            first = pl.multiple_of(t * TILE, TILE)
            w = w_all[source, pl.ds(first, TILE), :]
            at = pl.ds(pl.multiple_of(start + first, 16), TILE)
            live_w[at, :] = jnp.where(row < count - first, w.astype(jnp.float32),
                                      0.0).astype(w.dtype)
            m = m_all[source, :, pl.ds(first, TILE)]
            m = pltpu.roll(jnp.where(field == 0, base - m, m), shift, 1)
            here = lax.div(start, TILE) + t
            live_m[here] = jnp.where(lane >= shift, m, live_m[here])
            live_m[here + 1] = jnp.where(lane < shift, m, live_m[here + 1])
            return c

        lax.fori_loop(0, (count + TILE - 1) // TILE, put, 0)
        return start + ((count + 15) // 16) * 16

    total = lax.fori_loop(0, sources, pack, jnp.int32(0))
    live_w[pl.ds(pl.multiple_of(total, 16), chunk), :] = jnp.zeros((chunk, columns), live_w.dtype)
    chunks = (total + chunk - 1) // chunk

    gy = [(lax.broadcasted_iota(jnp.int32, (8, TILE), 0).astype(jnp.float32) + (8 * e + 0.5)) / GY
          for e in range(GY // 8)]
    rises = lax.broadcasted_iota(jnp.int32, (group, TILE), 0)

    def make(slot, block, first_level):
        heights = (rises + first_level).astype(jnp.float32)
        ivl = qtab[0, pl.ds(first_level, group), :]
        scale = qtab[1, pl.ds(first_level, group), :]
        for h in range(parts):
            m = live_m[block * parts + h]
            sep = (heights - m[2:3]) * ivl
            qs = (1.0 + sep * sep) * scale
            xs = [jnp.broadcast_to(m[0:1] + i / GX, (8, TILE)) for i in range(half_x)]
            ys = [g - m[1:2] for g in gy]
            y2s = [y * y for y in ys]
            for r in range(group):
                tv = tabs[0, first_level + r]
                td = tabs[1, first_level + r]
                t0 = tabs[2, first_level + r]
                q = jnp.broadcast_to(qs[r:r + 1], (8, TILE))
                vs = [y * tv for y in ys]
                ds = [y2 * td + t0 for y2 in y2s]
                for i in range(half_x):
                    done = []
                    for v, d in zip(vs, ds):
                        w = xs[i] + v
                        z = w * w + d
                        done.append(pl.reciprocal(z * z * q, approx=True))
                    at = r * half + i * GY
                    cover[slot, h, at:at + GY, :] = jnp.concatenate(
                        done, axis=0).astype(jnp.bfloat16)

    def use(slot, block, first_level):
        w = live_w[pl.ds(pl.multiple_of(block * chunk, chunk), chunk), :]
        at = pl.ds(pl.multiple_of(first_level * half, group * half), group * half)
        left = jnp.concatenate([cover[slot, h] for h in range(parts)], axis=1)
        acc[at, :] += jnp.dot(left, w, preferred_element_type=jnp.float32)

    turns = levels // (2 * group)

    def turn(step, c):
        block = lax.div(step, turns)
        level = pl.multiple_of(lax.rem(step, turns) * (2 * group), 2 * group)
        before = jnp.maximum(step - 1, 0)
        use(1, lax.div(before, turns), lax.rem(before, turns) * (2 * group) + group)
        make(0, block, level)
        use(0, block, level)
        make(1, block, level + group)
        return c

    lax.fori_loop(0, chunks * turns, turn, 0)
    use(1, chunks - 1, levels - group)

    share = levels // 2
    sect = sect_ref[0]
    bal = jnp.concatenate([bal_ref[pl.ds(pl.multiple_of(sect * share, share), share), :],
                           bal_ref[pl.ds(pl.multiple_of((1 - sect) * share, share), share), :]],
                          axis=0)
    bal_hi = bal.astype(jnp.bfloat16)
    bal_lo = (bal - bal_hi.astype(jnp.float32)).astype(jnp.bfloat16)
    left = jnp.concatenate([bal_hi, bal_lo], axis=0)

    def balance(n, c):
        for m in range(4):
            g = n * 8 + m * 2
            a = jnp.concatenate([acc[pl.ds(g + e, levels, stride=half), :] for e in range(2)],
                                axis=1)
            hi = a.astype(jnp.bfloat16)
            lo = (a - hi.astype(jnp.float32)).astype(jnp.bfloat16)
            inc = jnp.dot(left, hi, preferred_element_type=jnp.float32)
            inc = (inc[:levels] + inc[levels:]
                   + jnp.dot(bal_hi, lo, preferred_element_type=jnp.float32))
            for e in range(2):
                at = pl.ds(g + e, share, stride=half)
                mine[at, :] = inc[:share, e * columns:(e + 1) * columns]
                other_ref[at, :] = inc[share:, e * columns:(e + 1) * columns]
        return c

    lax.fori_loop(0, half // 8, balance, 0)
    place = pltpu.make_async_copy(mine.reshape(share, half, columns),
                                  part_ref.at[:, pl.ds(sect * half, half), :], out_sem)
    place.start()
    place.wait()


def spread(sect, weights, metas, length_x, length_y, tilt, vert_len, balance):
    slots, sections, rows, columns = weights.shape
    sources = slots * sections
    weights = weights.reshape(sources, rows, columns)
    metas = metas.reshape(sources, META, rows)
    levels = balance.shape[0]
    half_x = GX // sections
    half = half_x * GY
    chunk = 4 * TILE
    live = sources * rows + chunk
    vmem = pl.BlockSpec(memory_space=pltpu.VMEM)
    hbm = pl.BlockSpec(memory_space=pltpu.HBM)
    out = jax.ShapeDtypeStruct((levels // 2 * half, columns), jnp.float32)
    whole = jax.ShapeDtypeStruct((levels // 2, sections * half, columns), jnp.float32)
    line = pltpu.VMEM((1, levels), jnp.float32)
    return pl.pallas_call(
        functools.partial(spread_kernel, levels, half_x),
        out_shape=(whole, out),
        in_specs=[pl.BlockSpec(memory_space=pltpu.SMEM)] + [hbm] * 7,
        out_specs=(hbm, vmem),
        scratch_shapes=[
            pltpu.VMEM((levels * half, columns), jnp.float32),
            pltpu.VMEM((levels // 2 * half, columns), jnp.float32),
            pltpu.SemaphoreType.DMA,
            pltpu.VMEM((sources, rows, columns), jnp.bfloat16),
            pltpu.VMEM((sources, META, rows), jnp.float32),
            pltpu.SMEM((sources, META, TILE), jnp.float32),
            line, line, line, line,
            pltpu.VMEM((levels, levels), jnp.float32),
            pltpu.VMEM((live, columns), jnp.bfloat16),
            pltpu.VMEM((live // TILE + 1, META, TILE), jnp.float32),
            pltpu.VMEM((2, chunk // TILE, 8 * half, TILE), jnp.bfloat16),
            pltpu.VMEM((3, levels, 8, TILE), jnp.float32),
            pltpu.VMEM((2, levels, TILE), jnp.float32),
            pltpu.SemaphoreType.DMA((8,)),
        ],
        compiler_params=pltpu.CompilerParams(vmem_limit_bytes=VMEM_BYTES),
        name="spread_and_balance",
    )(sect, weights, metas, length_x, length_y, tilt, vert_len, balance)


def put_in_kernel(sect_ref, part_ref, came_ref, out_ref, sem):
    half = came_ref.shape[1]
    copy = pltpu.make_async_copy(
        came_ref, out_ref.at[:, pl.ds((1 - sect_ref[0]) * half, half), :], sem)
    copy.start()
    copy.wait()


def put_in(sect, part, came):
    hbm = pl.BlockSpec(memory_space=pltpu.HBM)
    return pl.pallas_call(
        put_in_kernel,
        out_shape=jax.ShapeDtypeStruct(part.shape, part.dtype),
        in_specs=[pl.BlockSpec(memory_space=pltpu.SMEM), hbm, hbm],
        out_specs=hbm,
        scratch_shapes=[pltpu.SemaphoreType.DMA],
        input_output_aliases={1: 0},
        name="put_in",
    )(sect, part, came)


def shards(blocks, obs_weight, obs_frac, obs_cell, obs_level, obs_count, reach,
           length_x, length_y, tilt, vert_len, balance):
    levels = balance.shape[0]
    columns = obs_weight.shape[3]
    sections = lax.axis_size("sect")
    weights, metas = gather(blocks, obs_weight[0, 0], obs_frac[0, 0], obs_cell[0], obs_level[0],
                            obs_count, reach)
    sect = lax.axis_index("sect").reshape(1).astype(jnp.int32)
    part, other = spread(sect, weights, metas, length_x[None], length_y[None], tilt[None],
                         vert_len[None], balance)
    came = lax.ppermute(other.reshape(levels // sections, -1, columns), "sect", [(0, 1), (1, 0)])
    return put_in(sect, part, came)


def solution(mesh):
    placed = (
        P(("date", "blk"), "sect", None, None),
        P(("date", "blk"), "sect", None, None),
        P(("date", "blk"), "sect", None),
        P(("date", "blk"), "sect", None),
        P(("date", "blk"), "sect"),
        P(("date", "blk"), None),
        P(),
        P(),
        P(),
        P(),
        P(),
    )
    return jax.shard_map(
        functools.partial(shards, mesh.shape["blk"]),
        mesh=mesh,
        in_specs=placed,
        out_specs=P("sect", ("date", "blk"), None),
        check_vma=False,
    )
```

```python
import functools

import jax
import jax.numpy as jnp
from jax import lax
from jax.experimental import pallas as pl
from jax.experimental.pallas import tpu as pltpu
from jax.sharding import PartitionSpec as P

GX = 8
GY = 16
REACH = 3
TILE = 128
META = 4
VMEM_BYTES = 60 * 1024 * 1024
MESH = pl.DeviceIdType.MESH


def gather_kernel(blocks, w_ref, frac_ref, cell_ref, level_ref, count_ref, reach_ref,
                  wo_ref, mo_ref, meta, d_send, d_recv, r_send, r_recv, s_send, s_recv, own_sem):
    blk = lax.axis_index("blk")
    sect = lax.axis_index("sect")
    sibling = {"sect": 1 - sect}
    toward = 1 - 2 * lax.rem(blk, 2)
    rows = w_ref.shape[0]
    cut = rows // 2

    def at(k):
        return {"blk": lax.rem(blk + k + blocks, blocks)}

    direct = [2, -2, toward, -3 * toward]
    origin = [2, -2, -toward, 3 * toward]
    barrier = pltpu.get_barrier_semaphore()
    for k in direct:
        pl.semaphore_signal(barrier, inc=1, device_id=at(k), device_id_type=MESH)
    pl.semaphore_signal(barrier, inc=1, device_id=sibling, device_id_type=MESH)

    cell = cell_ref[...]
    frac = frac_ref[...].astype(jnp.float32)
    meta[0:1, :] = ((cell // GY).astype(jnp.float32) + frac[0:1]) / GX
    meta[1:2, :] = ((cell % GY).astype(jnp.float32) + frac[1:2]) / GY
    meta[2:3, :] = level_ref[...].astype(jnp.float32)
    lane = lax.broadcasted_iota(jnp.int32, cell.shape, 1)
    reach = reach_ref[...].astype(jnp.float32)
    meta[3:4, :] = jnp.where(lane == 0, count_ref[...].astype(jnp.float32),
                             jnp.where(lane == 1, reach[:, 0:1], reach[:, 1:2]))

    pl.semaphore_wait(barrier, len(direct) + 1)

    def kept(k, part):
        if part == 0:
            return mo_ref.at[k + REACH, sect]
        return wo_ref.at[k + REACH, sect, pl.ds((part - 1) * cut, cut)]

    def mine(part):
        return meta if part == 0 else w_ref.at[pl.ds((part - 1) * cut, cut)]

    def copy(src, k, part, send, recv, n, target):
        return pltpu.make_async_remote_copy(
            src_ref=src, dst_ref=kept(k, part), send_sem=send.at[n, part],
            recv_sem=recv.at[n, part], device_id=target, device_id_type=MESH)

    sent = []

    def launch(*what):
        c = copy(*what)
        c.start()
        sent.append(c)

    def share(src, k, part, n):
        launch(src, k, part, s_send, s_recv, n, sibling)

    for part in range(3):
        for n in range(3):
            launch(mine(part), direct[n], part, d_send, d_recv, n, at(direct[n]))
    for part in range(3):
        share(mine(part), 0, part, 6)
    for part in range(3):
        launch(mine(part), direct[3], part, d_send, d_recv, 3, at(direct[3]))
    own = [pltpu.make_async_copy(mine(part), kept(0, part), own_sem.at[part]) for part in range(3)]
    for c in own:
        c.start()

    def arrive(k, part, recv, n):
        copy(kept(k, part), k, part, d_send, recv, n, sibling).wait_recv()

    for part in range(3):
        for n in range(2):
            k = origin[n]
            arrive(k, part, d_recv, n)
            launch(kept(k, part), toward + k, part, r_send, r_recv, n, at(toward))
            share(kept(k, part), k, part, n)
        arrive(origin[2], part, d_recv, 2)
        share(kept(origin[2], part), origin[2], part, 2)
    for part in range(3):
        arrive(origin[3], part, d_recv, 3)
        share(kept(origin[3], part), origin[3], part, 3)
        for n in range(2):
            k = origin[n] - toward
            arrive(k, part, r_recv, n)
            share(kept(k, part), k, part, 4 + n)
    for c in own:
        c.wait()
    for c in sent:
        c.wait_send()
    for n in range(7):
        for part in range(3):
            arrive(0, part, s_recv, n)


def gather(blocks, weight, frac, cell, level, count, reach):
    rows, columns = weight.shape
    slots = 2 * REACH + 1
    sems = [pltpu.SemaphoreType.DMA((n, 3)) for n in (4, 4, 2, 2, slots, slots)]
    vmem = pl.BlockSpec(memory_space=pltpu.VMEM)
    hbm = pl.BlockSpec(memory_space=pl.ANY)
    return pl.pallas_call(
        functools.partial(gather_kernel, blocks),
        out_shape=(jax.ShapeDtypeStruct((slots, 2, rows, columns), weight.dtype),
                   jax.ShapeDtypeStruct((slots, 2, META, rows), jnp.float32)),
        in_specs=[hbm, vmem, vmem, vmem, vmem, vmem],
        out_specs=(hbm, hbm),
        scratch_shapes=[pltpu.VMEM((META, rows), jnp.float32)] + sems
        + [pltpu.SemaphoreType.DMA((3,))],
        compiler_params=pltpu.CompilerParams(collective_id=0, has_side_effects=True),
        name="gather_packets",
    )(weight, frac, cell, level, count, reach)


def spread_kernel(levels, half_x, sect_ref, w_hbm, m_hbm, lx_hbm, ly_hbm, tilt_hbm, vl_hbm,
                  bal_hbm, part_ref, other_ref, acc, mine, out_sem, w_all, m_all, info, lx_ref, ly_ref, tilt_ref,
                  vl_ref, bal_ref, live_w, live_m, cover, tabs, qtab, sems):
    sources, rows, columns = w_all.shape
    half = half_x * GY
    group = 8
    parts = cover.shape[1]
    chunk = parts * TILE
    wanted = [(m_hbm.at[:, :, pl.ds(0, TILE)], info), (lx_hbm, lx_ref), (ly_hbm, ly_ref),
              (tilt_hbm, tilt_ref), (vl_hbm, vl_ref), (bal_hbm, bal_ref), (m_hbm, m_all),
              (w_hbm, w_all)]
    fetches = [pltpu.make_async_copy(src, dst, sems.at[n]) for n, (src, dst) in enumerate(wanted)]
    for fetch in fetches:
        fetch.start()
    acc[...] = jnp.zeros_like(acc)
    live_m[...] = jnp.zeros_like(live_m)
    cover[1] = jnp.zeros(cover.shape[1:], cover.dtype)
    for fetch in fetches[:6]:
        fetch.wait()

    eye = (lax.broadcasted_iota(jnp.int32, (levels, levels), 0)
           == lax.broadcasted_iota(jnp.int32, (levels, levels), 1))

    def column(ref):
        wide = jnp.broadcast_to(ref[...], (levels, levels))
        return jnp.sum(jnp.where(eye, wide, 0.0), axis=1, keepdims=True)

    lx, ly, tilt, vl = column(lx_ref), column(ly_ref), column(tilt_ref), column(vl_ref)
    ratio = lx / ly
    ilx2 = 1.0 / (lx * lx)
    entries = [tilt * ratio, (1.0 - tilt * tilt) * ratio * ratio, lx * lx]
    for n, entry in enumerate(entries):
        tabs[n] = jnp.broadcast_to(entry[:, :, None], (levels, 8, TILE))
    qtab[0] = jnp.broadcast_to(1.0 / vl, (levels, TILE))
    qtab[1] = jnp.broadcast_to(ilx2 * ilx2, (levels, TILE))

    for fetch in fetches[6:]:
        fetch.wait()
    x0 = sect_ref[0].astype(jnp.float32) * (half_x / GX) + 0.5 / GX
    row = lax.broadcasted_iota(jnp.int32, (TILE, columns), 0)
    lane = lax.broadcasted_iota(jnp.int32, (META, TILE), 1)
    field = lax.broadcasted_iota(jnp.int32, (META, TILE), 0)

    def pack(source, start):
        k = lax.div(source, sources // (2 * REACH + 1)) - REACH
        count = info[source, 3, 0].astype(jnp.int32)
        low = info[source, 3, 1].astype(jnp.int32)
        high = info[source, 3, 2].astype(jnp.int32)
        count = jnp.where((k <= high) & (-k <= low), count, 0)
        shift = lax.rem(start, TILE)
        base = k.astype(jnp.float32) + x0

        def put(t, c):
            first = pl.multiple_of(t * TILE, TILE)
            w = w_all[source, pl.ds(first, TILE), :]
            at = pl.ds(pl.multiple_of(start + first, 16), TILE)
            live_w[at, :] = jnp.where(row < count - first, w.astype(jnp.float32),
                                      0.0).astype(w.dtype)
            m = m_all[source, :, pl.ds(first, TILE)]
            m = pltpu.roll(jnp.where(field == 0, base - m, m), shift, 1)
            here = lax.div(start, TILE) + t
            live_m[here] = jnp.where(lane >= shift, m, live_m[here])
            live_m[here + 1] = jnp.where(lane < shift, m, live_m[here + 1])
            return c

        lax.fori_loop(0, (count + TILE - 1) // TILE, put, 0)
        return start + ((count + 15) // 16) * 16

    total = lax.fori_loop(0, sources, pack, jnp.int32(0))
    live_w[pl.ds(pl.multiple_of(total, 16), chunk), :] = jnp.zeros((chunk, columns), live_w.dtype)
    chunks = (total + chunk - 1) // chunk

    gy = [(lax.broadcasted_iota(jnp.int32, (8, TILE), 0).astype(jnp.float32) + (8 * e + 0.5)) / GY
          for e in range(GY // 8)]
    rises = lax.broadcasted_iota(jnp.int32, (group, TILE), 0)

    def make(slot, block, first_level):
        heights = (rises + first_level).astype(jnp.float32)
        ivl = qtab[0, pl.ds(first_level, group), :]
        scale = qtab[1, pl.ds(first_level, group), :]
        for h in range(parts):
            m = live_m[block * parts + h]
            sep = (heights - m[2:3]) * ivl
            qs = (1.0 + sep * sep) * scale
            xs = [jnp.broadcast_to(m[0:1] + i / GX, (8, TILE)) for i in range(half_x)]
            ys = [g - m[1:2] for g in gy]
            y2s = [y * y for y in ys]
            for r in range(group):
                tv = tabs[0, first_level + r]
                td = tabs[1, first_level + r]
                t0 = tabs[2, first_level + r]
                q = jnp.broadcast_to(qs[r:r + 1], (8, TILE))
                vs = [y * tv for y in ys]
                ds = [y2 * td + t0 for y2 in y2s]
                for i in range(half_x):
                    done = []
                    for v, d in zip(vs, ds):
                        w = xs[i] + v
                        z = w * w + d
                        done.append(pl.reciprocal(z * z * q, approx=True))
                    at = r * half + i * GY
                    cover[slot, h, at:at + GY, :] = jnp.concatenate(
                        done, axis=0).astype(jnp.bfloat16)

    def use(slot, block, first_level):
        w = live_w[pl.ds(pl.multiple_of(block * chunk, chunk), chunk), :]
        at = pl.ds(pl.multiple_of(first_level * half, group * half), group * half)
        terms = []
        for h in range(0, parts, 2):
            left = jnp.concatenate([cover[slot, h], cover[slot, h + 1]], axis=1)
            terms.append(jnp.dot(left, w[h * TILE:(h + 2) * TILE],
                                 preferred_element_type=jnp.float32))
        acc[at, :] += sum(terms[1:], terms[0])

    turns = levels // (2 * group)

    def turn(step, c):
        block = lax.div(step, turns)
        level = pl.multiple_of(lax.rem(step, turns) * (2 * group), 2 * group)
        before = jnp.maximum(step - 1, 0)
        use(1, lax.div(before, turns), lax.rem(before, turns) * (2 * group) + group)
        make(0, block, level)
        use(0, block, level)
        make(1, block, level + group)
        return c

    lax.fori_loop(0, chunks * turns, turn, 0)
    use(1, chunks - 1, levels - group)

    share = levels // 2
    sect = sect_ref[0]
    bal = jnp.concatenate([bal_ref[pl.ds(pl.multiple_of(sect * share, share), share), :],
                           bal_ref[pl.ds(pl.multiple_of((1 - sect) * share, share), share), :]],
                          axis=0)
    bal_hi = bal.astype(jnp.bfloat16)
    bal_lo = (bal - bal_hi.astype(jnp.float32)).astype(jnp.bfloat16)
    left = jnp.concatenate([bal_hi, bal_lo], axis=0)

    def balance(n, c):
        for m in range(4):
            g = n * 8 + m * 2
            a = jnp.concatenate([acc[pl.ds(g + e, levels, stride=half), :] for e in range(2)],
                                axis=1)
            hi = a.astype(jnp.bfloat16)
            lo = (a - hi.astype(jnp.float32)).astype(jnp.bfloat16)
            inc = jnp.dot(left, hi, preferred_element_type=jnp.float32)
            inc = (inc[:levels] + inc[levels:]
                   + jnp.dot(bal_hi, lo, preferred_element_type=jnp.float32))
            for e in range(2):
                at = pl.ds(g + e, share, stride=half)
                mine[at, :] = inc[:share, e * columns:(e + 1) * columns]
                other_ref[at, :] = inc[share:, e * columns:(e + 1) * columns]
        return c

    lax.fori_loop(0, half // 8, balance, 0)
    place = pltpu.make_async_copy(mine.reshape(share, half, columns),
                                  part_ref.at[:, pl.ds(sect * half, half), :], out_sem)
    place.start()
    place.wait()


def spread(sect, weights, metas, length_x, length_y, tilt, vert_len, balance):
    slots, sections, rows, columns = weights.shape
    sources = slots * sections
    weights = weights.reshape(sources, rows, columns)
    metas = metas.reshape(sources, META, rows)
    levels = balance.shape[0]
    half_x = GX // sections
    half = half_x * GY
    chunk = 4 * TILE
    live = sources * rows + chunk
    vmem = pl.BlockSpec(memory_space=pltpu.VMEM)
    hbm = pl.BlockSpec(memory_space=pltpu.HBM)
    out = jax.ShapeDtypeStruct((levels // 2 * half, columns), jnp.float32)
    whole = jax.ShapeDtypeStruct((levels // 2, sections * half, columns), jnp.float32)
    line = pltpu.VMEM((1, levels), jnp.float32)
    return pl.pallas_call(
        functools.partial(spread_kernel, levels, half_x),
        out_shape=(whole, out),
        in_specs=[pl.BlockSpec(memory_space=pltpu.SMEM)] + [hbm] * 7,
        out_specs=(hbm, vmem),
        scratch_shapes=[
            pltpu.VMEM((levels * half, columns), jnp.float32),
            pltpu.VMEM((levels // 2 * half, columns), jnp.float32),
            pltpu.SemaphoreType.DMA,
            pltpu.VMEM((sources, rows, columns), jnp.bfloat16),
            pltpu.VMEM((sources, META, rows), jnp.float32),
            pltpu.SMEM((sources, META, TILE), jnp.float32),
            line, line, line, line,
            pltpu.VMEM((levels, levels), jnp.float32),
            pltpu.VMEM((live, columns), jnp.bfloat16),
            pltpu.VMEM((live // TILE + 1, META, TILE), jnp.float32),
            pltpu.VMEM((2, chunk // TILE, 8 * half, TILE), jnp.bfloat16),
            pltpu.VMEM((3, levels, 8, TILE), jnp.float32),
            pltpu.VMEM((2, levels, TILE), jnp.float32),
            pltpu.SemaphoreType.DMA((8,)),
        ],
        compiler_params=pltpu.CompilerParams(vmem_limit_bytes=VMEM_BYTES),
        name="spread_and_balance",
    )(sect, weights, metas, length_x, length_y, tilt, vert_len, balance)


def put_in_kernel(sect_ref, part_ref, came_ref, out_ref):
    out_ref[...] = came_ref[...]


def put_in(sect, part, came):
    levels, half, columns = came.shape
    steps = 4
    block = (levels // steps, half, columns)
    return pl.pallas_call(
        put_in_kernel,
        out_shape=jax.ShapeDtypeStruct(part.shape, part.dtype),
        grid_spec=pltpu.PrefetchScalarGridSpec(
            num_scalar_prefetch=1,
            grid=(steps,),
            in_specs=[pl.BlockSpec(memory_space=pltpu.HBM),
                      pl.BlockSpec(block, lambda i, sect: (i, 0, 0))],
            out_specs=pl.BlockSpec(block, lambda i, sect: (i, 1 - sect[0], 0)),
        ),
        input_output_aliases={1: 0},
        name="put_in",
    )(sect, part, came)


def shards(blocks, obs_weight, obs_frac, obs_cell, obs_level, obs_count, reach,
           length_x, length_y, tilt, vert_len, balance):
    levels = balance.shape[0]
    columns = obs_weight.shape[3]
    sections = lax.axis_size("sect")
    weights, metas = gather(blocks, obs_weight[0, 0], obs_frac[0, 0], obs_cell[0], obs_level[0],
                            obs_count, reach)
    sect = lax.axis_index("sect").reshape(1).astype(jnp.int32)
    part, other = spread(sect, weights, metas, length_x[None], length_y[None], tilt[None],
                         vert_len[None], balance)
    came = lax.ppermute(other.reshape(levels // sections, -1, columns), "sect", [(0, 1), (1, 0)])
    return put_in(sect, part, came)


def solution(mesh):
    placed = (
        P(("date", "blk"), "sect", None, None),
        P(("date", "blk"), "sect", None, None),
        P(("date", "blk"), "sect", None),
        P(("date", "blk"), "sect", None),
        P(("date", "blk"), "sect"),
        P(("date", "blk"), None),
        P(),
        P(),
        P(),
        P(),
        P(),
    )
    return jax.shard_map(
        functools.partial(shards, mesh.shape["blk"]),
        mesh=mesh,
        in_specs=placed,
        out_specs=P("sect", ("date", "blk"), None),
        check_vma=False,
    )
```

```python
import functools

import jax
import jax.numpy as jnp
from jax import lax
from jax.experimental import pallas as pl
from jax.experimental.pallas import tpu as pltpu
from jax.sharding import PartitionSpec as P

GX = 8
GY = 16
REACH = 3
TILE = 128
META = 4
VMEM_BYTES = 60 * 1024 * 1024
MESH = pl.DeviceIdType.MESH


def gather_kernel(blocks, w_ref, frac_ref, cell_ref, level_ref, count_ref, reach_ref,
                  wo_ref, mo_ref, meta, d_send, d_recv, r_send, r_recv, s_send, s_recv, own_sem):
    blk = lax.axis_index("blk")
    sect = lax.axis_index("sect")
    sibling = {"sect": 1 - sect}
    toward = 1 - 2 * lax.rem(blk, 2)
    rows = w_ref.shape[0]
    cut = rows // 2

    def at(k):
        return {"blk": lax.rem(blk + k + blocks, blocks)}

    direct = [2, -2, toward, -3 * toward]
    origin = [2, -2, -toward, 3 * toward]
    barrier = pltpu.get_barrier_semaphore()
    for k in direct:
        pl.semaphore_signal(barrier, inc=1, device_id=at(k), device_id_type=MESH)
    pl.semaphore_signal(barrier, inc=1, device_id=sibling, device_id_type=MESH)

    cell = cell_ref[...]
    frac = frac_ref[...].astype(jnp.float32)
    meta[0:1, :] = ((cell // GY).astype(jnp.float32) + frac[0:1]) / GX
    meta[1:2, :] = ((cell % GY).astype(jnp.float32) + frac[1:2]) / GY
    meta[2:3, :] = level_ref[...].astype(jnp.float32)
    lane = lax.broadcasted_iota(jnp.int32, cell.shape, 1)
    reach = reach_ref[...].astype(jnp.float32)
    meta[3:4, :] = jnp.where(lane == 0, count_ref[...].astype(jnp.float32),
                             jnp.where(lane == 1, reach[:, 0:1], reach[:, 1:2]))

    pl.semaphore_wait(barrier, len(direct) + 1)

    def kept(k, part):
        if part == 0:
            return mo_ref.at[k + REACH, sect]
        return wo_ref.at[k + REACH, sect, pl.ds((part - 1) * cut, cut)]

    def mine(part):
        return meta if part == 0 else w_ref.at[pl.ds((part - 1) * cut, cut)]

    def copy(src, k, part, send, recv, n, target):
        return pltpu.make_async_remote_copy(
            src_ref=src, dst_ref=kept(k, part), send_sem=send.at[n, part],
            recv_sem=recv.at[n, part], device_id=target, device_id_type=MESH)

    sent = []

    def launch(*what):
        c = copy(*what)
        c.start()
        sent.append(c)

    def share(src, k, part, n):
        launch(src, k, part, s_send, s_recv, n, sibling)

    for part in range(3):
        for n in range(3):
            launch(mine(part), direct[n], part, d_send, d_recv, n, at(direct[n]))
    for part in range(3):
        share(mine(part), 0, part, 6)
    for part in range(3):
        launch(mine(part), direct[3], part, d_send, d_recv, 3, at(direct[3]))
    own = [pltpu.make_async_copy(mine(part), kept(0, part), own_sem.at[part]) for part in range(3)]
    for c in own:
        c.start()

    def arrive(k, part, recv, n):
        copy(kept(k, part), k, part, d_send, recv, n, sibling).wait_recv()

    for part in range(3):
        for n in range(2):
            k = origin[n]
            arrive(k, part, d_recv, n)
            launch(kept(k, part), toward + k, part, r_send, r_recv, n, at(toward))
            share(kept(k, part), k, part, n)
        arrive(origin[2], part, d_recv, 2)
        share(kept(origin[2], part), origin[2], part, 2)
    for part in range(3):
        arrive(origin[3], part, d_recv, 3)
        share(kept(origin[3], part), origin[3], part, 3)
        for n in range(2):
            k = origin[n] - toward
            arrive(k, part, r_recv, n)
            share(kept(k, part), k, part, 4 + n)
    for c in own:
        c.wait()
    for c in sent:
        c.wait_send()
    for n in range(7):
        for part in range(3):
            arrive(0, part, s_recv, n)


def gather(blocks, weight, frac, cell, level, count, reach):
    rows, columns = weight.shape
    slots = 2 * REACH + 1
    sems = [pltpu.SemaphoreType.DMA((n, 3)) for n in (4, 4, 2, 2, slots, slots)]
    vmem = pl.BlockSpec(memory_space=pltpu.VMEM)
    hbm = pl.BlockSpec(memory_space=pl.ANY)
    return pl.pallas_call(
        functools.partial(gather_kernel, blocks),
        out_shape=(jax.ShapeDtypeStruct((slots, 2, rows, columns), weight.dtype),
                   jax.ShapeDtypeStruct((slots, 2, META, rows), jnp.float32)),
        in_specs=[hbm, vmem, vmem, vmem, vmem, vmem],
        out_specs=(hbm, hbm),
        scratch_shapes=[pltpu.VMEM((META, rows), jnp.float32)] + sems
        + [pltpu.SemaphoreType.DMA((3,))],
        compiler_params=pltpu.CompilerParams(collective_id=0, has_side_effects=True),
        name="gather_packets",
    )(weight, frac, cell, level, count, reach)


def spread_kernel(levels, half_x, sect_ref, w_hbm, m_hbm, lx_hbm, ly_hbm, tilt_hbm, vl_hbm,
                  bal_hbm, part_ref, other_ref, acc, mine, out_sem, w_all, m_all, info, lx_ref, ly_ref, tilt_ref,
                  vl_ref, bal_ref, live_w, live_m, cover, tabs, qtab, sems):
    sources, rows, columns = w_all.shape
    half = half_x * GY
    group = 8
    parts = cover.shape[1]
    chunk = parts * TILE
    wanted = [(m_hbm.at[:, :, pl.ds(0, TILE)], info), (lx_hbm, lx_ref), (ly_hbm, ly_ref),
              (tilt_hbm, tilt_ref), (vl_hbm, vl_ref), (bal_hbm, bal_ref), (m_hbm, m_all),
              (w_hbm, w_all)]
    fetches = [pltpu.make_async_copy(src, dst, sems.at[n]) for n, (src, dst) in enumerate(wanted)]
    for fetch in fetches:
        fetch.start()
    acc[...] = jnp.zeros_like(acc)
    live_m[...] = jnp.zeros_like(live_m)
    cover[1] = jnp.zeros(cover.shape[1:], cover.dtype)
    for fetch in fetches[:6]:
        fetch.wait()

    eye = (lax.broadcasted_iota(jnp.int32, (levels, levels), 0)
           == lax.broadcasted_iota(jnp.int32, (levels, levels), 1))

    def column(ref):
        wide = jnp.broadcast_to(ref[...], (levels, levels))
        return jnp.sum(jnp.where(eye, wide, 0.0), axis=1, keepdims=True)

    lx, ly, tilt, vl = column(lx_ref), column(ly_ref), column(tilt_ref), column(vl_ref)
    ratio = lx / ly
    ilx2 = 1.0 / (lx * lx)
    entries = [tilt * ratio, (1.0 - tilt * tilt) * ratio * ratio, lx * lx]
    for n, entry in enumerate(entries):
        tabs[n] = jnp.broadcast_to(entry[:, :, None], (levels, 8, TILE))
    qtab[0] = jnp.broadcast_to(1.0 / vl, (levels, TILE))
    qtab[1] = jnp.broadcast_to(ilx2 * ilx2, (levels, TILE))

    for fetch in fetches[6:]:
        fetch.wait()
    x0 = sect_ref[0].astype(jnp.float32) * (half_x / GX) + 0.5 / GX
    row = lax.broadcasted_iota(jnp.int32, (TILE, columns), 0)
    lane = lax.broadcasted_iota(jnp.int32, (META, TILE), 1)
    field = lax.broadcasted_iota(jnp.int32, (META, TILE), 0)

    def pack(source, start):
        k = lax.div(source, sources // (2 * REACH + 1)) - REACH
        count = info[source, 3, 0].astype(jnp.int32)
        low = info[source, 3, 1].astype(jnp.int32)
        high = info[source, 3, 2].astype(jnp.int32)
        count = jnp.where((k <= high) & (-k <= low), count, 0)
        shift = lax.rem(start, TILE)
        base = k.astype(jnp.float32) + x0

        def put(t, c):
            first = pl.multiple_of(t * TILE, TILE)
            w = w_all[source, pl.ds(first, TILE), :]
            at = pl.ds(pl.multiple_of(start + first, 16), TILE)
            live_w[at, :] = jnp.where(row < count - first, w.astype(jnp.float32), 0.0)
            m = m_all[source, :, pl.ds(first, TILE)]
            m = pltpu.roll(jnp.where(field == 0, base - m, m), shift, 1)
            here = lax.div(start, TILE) + t
            live_m[here] = jnp.where(lane >= shift, m, live_m[here])
            live_m[here + 1] = jnp.where(lane < shift, m, live_m[here + 1])
            return c

        lax.fori_loop(0, (count + TILE - 1) // TILE, put, 0)
        return start + ((count + 15) // 16) * 16

    total = lax.fori_loop(0, sources, pack, jnp.int32(0))
    live_w[pl.ds(pl.multiple_of(total, 16), chunk), :] = jnp.zeros((chunk, columns), live_w.dtype)
    chunks = (total + chunk - 1) // chunk

    gy = [(lax.broadcasted_iota(jnp.int32, (8, TILE), 0).astype(jnp.float32) + (8 * e + 0.5)) / GY
          for e in range(GY // 8)]
    rises = lax.broadcasted_iota(jnp.int32, (group, TILE), 0)

    def make(slot, block, first_level):
        heights = (rises + first_level).astype(jnp.float32)
        ivl = qtab[0, pl.ds(first_level, group), :]
        scale = qtab[1, pl.ds(first_level, group), :]
        for h in range(parts):
            m = live_m[block * parts + h]
            sep = (heights - m[2:3]) * ivl
            qs = (1.0 + sep * sep) * scale
            xs = [jnp.broadcast_to(m[0:1] + i / GX, (8, TILE)) for i in range(half_x)]
            ys = [g - m[1:2] for g in gy]
            y2s = [y * y for y in ys]
            for r in range(group):
                tv = tabs[0, first_level + r]
                td = tabs[1, first_level + r]
                t0 = tabs[2, first_level + r]
                q = jnp.broadcast_to(qs[r:r + 1], (8, TILE))
                vs = [y * tv for y in ys]
                ds = [y2 * td + t0 for y2 in y2s]
                for i in range(half_x):
                    done = []
                    for v, d in zip(vs, ds):
                        w = xs[i] + v
                        z = w * w + d
                        done.append(pl.reciprocal(z * z * q, approx=True))
                    at = r * half + i * GY
                    cover[slot, h, at:at + GY, :] = jnp.concatenate(done, axis=0)

    def use(slot, block, first_level):
        w = live_w[pl.ds(pl.multiple_of(block * chunk, chunk), chunk), :]
        at = pl.ds(pl.multiple_of(first_level * half, group * half), group * half)
        terms = []
        for h in range(0, parts, 2):
            left = jnp.concatenate([cover[slot, h], cover[slot, h + 1]], axis=1)
            terms.append(jnp.dot(left, w[h * TILE:(h + 2) * TILE],
                                 precision=lax.Precision.DEFAULT,
                                 preferred_element_type=jnp.float32))
        acc[at, :] += sum(terms[1:], terms[0])

    turns = levels // (2 * group)

    def turn(step, c):
        block = lax.div(step, turns)
        level = pl.multiple_of(lax.rem(step, turns) * (2 * group), 2 * group)
        before = jnp.maximum(step - 1, 0)
        use(1, lax.div(before, turns), lax.rem(before, turns) * (2 * group) + group)
        make(0, block, level)
        use(0, block, level)
        make(1, block, level + group)
        return c

    lax.fori_loop(0, chunks * turns, turn, 0)
    use(1, chunks - 1, levels - group)

    share = levels // 2
    sect = sect_ref[0]
    bal = jnp.concatenate([bal_ref[pl.ds(pl.multiple_of(sect * share, share), share), :],
                           bal_ref[pl.ds(pl.multiple_of((1 - sect) * share, share), share), :]],
                          axis=0)
    bal_hi = bal.astype(jnp.bfloat16)
    bal_lo = (bal - bal_hi.astype(jnp.float32)).astype(jnp.bfloat16)
    left = jnp.concatenate([bal_hi, bal_lo], axis=0)

    def balance(n, c):
        for m in range(4):
            g = n * 8 + m * 2
            a = jnp.concatenate([acc[pl.ds(g + e, levels, stride=half), :] for e in range(2)],
                                axis=1)
            hi = a.astype(jnp.bfloat16)
            lo = (a - hi.astype(jnp.float32)).astype(jnp.bfloat16)
            inc = jnp.dot(left, hi, preferred_element_type=jnp.float32)
            inc = (inc[:levels] + inc[levels:]
                   + jnp.dot(bal_hi, lo, preferred_element_type=jnp.float32))
            for e in range(2):
                at = pl.ds(g + e, share, stride=half)
                mine[at, :] = inc[:share, e * columns:(e + 1) * columns]
                other_ref[at, :] = inc[share:, e * columns:(e + 1) * columns]
        return c

    lax.fori_loop(0, half // 8, balance, 0)
    place = pltpu.make_async_copy(mine.reshape(share, half, columns),
                                  part_ref.at[:, pl.ds(sect * half, half), :], out_sem)
    place.start()
    place.wait()


def spread(sect, weights, metas, length_x, length_y, tilt, vert_len, balance):
    slots, sections, rows, columns = weights.shape
    sources = slots * sections
    weights = weights.reshape(sources, rows, columns)
    metas = metas.reshape(sources, META, rows)
    levels = balance.shape[0]
    half_x = GX // sections
    half = half_x * GY
    chunk = 4 * TILE
    live = sources * rows + chunk
    vmem = pl.BlockSpec(memory_space=pltpu.VMEM)
    hbm = pl.BlockSpec(memory_space=pltpu.HBM)
    out = jax.ShapeDtypeStruct((levels // 2 * half, columns), jnp.float32)
    whole = jax.ShapeDtypeStruct((levels // 2, sections * half, columns), jnp.float32)
    line = pltpu.VMEM((1, levels), jnp.float32)
    return pl.pallas_call(
        functools.partial(spread_kernel, levels, half_x),
        out_shape=(whole, out),
        in_specs=[pl.BlockSpec(memory_space=pltpu.SMEM)] + [hbm] * 7,
        out_specs=(hbm, vmem),
        scratch_shapes=[
            pltpu.VMEM((levels * half, columns), jnp.float32),
            pltpu.VMEM((levels // 2 * half, columns), jnp.float32),
            pltpu.SemaphoreType.DMA,
            pltpu.VMEM((sources, rows, columns), jnp.bfloat16),
            pltpu.VMEM((sources, META, rows), jnp.float32),
            pltpu.SMEM((sources, META, TILE), jnp.float32),
            line, line, line, line,
            pltpu.VMEM((levels, levels), jnp.float32),
            pltpu.VMEM((live, columns), jnp.float32),
            pltpu.VMEM((live // TILE + 1, META, TILE), jnp.float32),
            pltpu.VMEM((2, chunk // TILE, 8 * half, TILE), jnp.float32),
            pltpu.VMEM((3, levels, 8, TILE), jnp.float32),
            pltpu.VMEM((2, levels, TILE), jnp.float32),
            pltpu.SemaphoreType.DMA((8,)),
        ],
        compiler_params=pltpu.CompilerParams(vmem_limit_bytes=VMEM_BYTES),
        name="spread_and_balance",
    )(sect, weights, metas, length_x, length_y, tilt, vert_len, balance)


def shards(blocks, obs_weight, obs_frac, obs_cell, obs_level, obs_count, reach,
           length_x, length_y, tilt, vert_len, balance):
    levels = balance.shape[0]
    columns = obs_weight.shape[3]
    sections = lax.axis_size("sect")
    weights, metas = gather(blocks, obs_weight[0, 0], obs_frac[0, 0], obs_cell[0], obs_level[0],
                            obs_count, reach)
    sect = lax.axis_index("sect").astype(jnp.int32)
    part, other = spread(sect.reshape(1), weights, metas, length_x[None], length_y[None], tilt[None],
                         vert_len[None], balance)
    came = lax.ppermute(other.reshape(levels // sections, -1, columns), "sect", [(0, 1), (1, 0)])
    return lax.dynamic_update_slice(part, came, (0, (1 - sect) * came.shape[1], 0))


def solution(mesh):
    placed = (
        P(("date", "blk"), "sect", None, None),
        P(("date", "blk"), "sect", None, None),
        P(("date", "blk"), "sect", None),
        P(("date", "blk"), "sect", None),
        P(("date", "blk"), "sect"),
        P(("date", "blk"), None),
        P(),
        P(),
        P(),
        P(),
        P(),
    )
    return jax.shard_map(
        functools.partial(shards, mesh.shape["blk"]),
        mesh=mesh,
        in_specs=placed,
        out_specs=P("sect", ("date", "blk"), None),
        check_vma=False,
    )
```

```python
import functools

import jax
import jax.numpy as jnp
from jax import lax
from jax.experimental import pallas as pl
from jax.experimental.pallas import tpu as pltpu
from jax.sharding import PartitionSpec as P

GX = 8
GY = 16
REACH = 3
TILE = 128
META = 4
VMEM_BYTES = 60 * 1024 * 1024
MESH = pl.DeviceIdType.MESH


def gather_kernel(blocks, w_ref, frac_ref, cell_ref, level_ref, count_ref, reach_ref,
                  wo_ref, mo_ref, meta, d_send, d_recv, r_send, r_recv, s_send, s_recv, own_sem):
    blk = lax.axis_index("blk")
    sect = lax.axis_index("sect")
    sibling = {"sect": 1 - sect}
    toward = 1 - 2 * lax.rem(blk, 2)
    rows = w_ref.shape[0]
    cut = rows // 2

    def at(k):
        return {"blk": lax.rem(blk + k + blocks, blocks)}

    direct = [2, -2, toward, -3 * toward]
    origin = [2, -2, -toward, 3 * toward]
    barrier = pltpu.get_barrier_semaphore()
    for k in direct:
        pl.semaphore_signal(barrier, inc=1, device_id=at(k), device_id_type=MESH)
    pl.semaphore_signal(barrier, inc=1, device_id=sibling, device_id_type=MESH)

    cell = cell_ref[...]
    frac = frac_ref[...].astype(jnp.float32)
    meta[0:1, :] = ((cell // GY).astype(jnp.float32) + frac[0:1]) / GX
    meta[1:2, :] = ((cell % GY).astype(jnp.float32) + frac[1:2]) / GY
    meta[2:3, :] = level_ref[...].astype(jnp.float32)
    lane = lax.broadcasted_iota(jnp.int32, cell.shape, 1)
    reach = reach_ref[...].astype(jnp.float32)
    meta[3:4, :] = jnp.where(lane == 0, count_ref[...].astype(jnp.float32),
                             jnp.where(lane == 1, reach[:, 0:1], reach[:, 1:2]))

    pl.semaphore_wait(barrier, len(direct) + 1)

    def kept(k, part):
        if part == 0:
            return mo_ref.at[k + REACH, sect]
        return wo_ref.at[k + REACH, sect, pl.ds((part - 1) * cut, cut)]

    def mine(part):
        return meta if part == 0 else w_ref.at[pl.ds((part - 1) * cut, cut)]

    def copy(src, k, part, send, recv, n, target):
        return pltpu.make_async_remote_copy(
            src_ref=src, dst_ref=kept(k, part), send_sem=send.at[n, part],
            recv_sem=recv.at[n, part], device_id=target, device_id_type=MESH)

    sent = []

    def launch(*what):
        c = copy(*what)
        c.start()
        sent.append(c)

    def share(src, k, part, n):
        launch(src, k, part, s_send, s_recv, n, sibling)

    for part in range(3):
        for n in range(3):
            launch(mine(part), direct[n], part, d_send, d_recv, n, at(direct[n]))
    for part in range(3):
        share(mine(part), 0, part, 6)
    for part in range(3):
        launch(mine(part), direct[3], part, d_send, d_recv, 3, at(direct[3]))
    own = [pltpu.make_async_copy(mine(part), kept(0, part), own_sem.at[part]) for part in range(3)]
    for c in own:
        c.start()

    def arrive(k, part, recv, n):
        copy(kept(k, part), k, part, d_send, recv, n, sibling).wait_recv()

    for part in range(3):
        for n in range(2):
            k = origin[n]
            arrive(k, part, d_recv, n)
            launch(kept(k, part), toward + k, part, r_send, r_recv, n, at(toward))
            share(kept(k, part), k, part, n)
        arrive(origin[2], part, d_recv, 2)
        share(kept(origin[2], part), origin[2], part, 2)
    for part in range(3):
        arrive(origin[3], part, d_recv, 3)
        share(kept(origin[3], part), origin[3], part, 3)
        for n in range(2):
            k = origin[n] - toward
            arrive(k, part, r_recv, n)
            share(kept(k, part), k, part, 4 + n)
    for c in own:
        c.wait()
    for c in sent:
        c.wait_send()
    for n in range(7):
        for part in range(3):
            arrive(0, part, s_recv, n)


def gather(blocks, weight, frac, cell, level, count, reach):
    rows, columns = weight.shape
    slots = 2 * REACH + 1
    sems = [pltpu.SemaphoreType.DMA((n, 3)) for n in (4, 4, 2, 2, slots, slots)]
    vmem = pl.BlockSpec(memory_space=pltpu.VMEM)
    hbm = pl.BlockSpec(memory_space=pl.ANY)
    return pl.pallas_call(
        functools.partial(gather_kernel, blocks),
        out_shape=(jax.ShapeDtypeStruct((slots, 2, rows, columns), weight.dtype),
                   jax.ShapeDtypeStruct((slots, 2, META, rows), jnp.float32)),
        in_specs=[hbm, vmem, vmem, vmem, vmem, vmem],
        out_specs=(hbm, hbm),
        scratch_shapes=[pltpu.VMEM((META, rows), jnp.float32)] + sems
        + [pltpu.SemaphoreType.DMA((3,))],
        compiler_params=pltpu.CompilerParams(collective_id=0, has_side_effects=True),
        name="gather_packets",
    )(weight, frac, cell, level, count, reach)


def spread_kernel(levels, half_x, sect_ref, w_hbm, m_hbm, lx_hbm, ly_hbm, tilt_hbm, vl_hbm,
                  bal_hbm, part_ref, other_ref, acc, mine, other, out_sem, w_all, m_all, info, lx_ref, ly_ref, tilt_ref,
                  vl_ref, bal_ref, live_w, live_m, cover, tabs, qtab, sems):
    sources, rows, columns = w_all.shape
    half = half_x * GY
    group = 8
    parts = cover.shape[1]
    chunk = parts * TILE
    wanted = [(m_hbm.at[:, :, pl.ds(0, TILE)], info), (lx_hbm, lx_ref), (ly_hbm, ly_ref),
              (tilt_hbm, tilt_ref), (vl_hbm, vl_ref), (bal_hbm, bal_ref), (m_hbm, m_all),
              (w_hbm, w_all)]
    fetches = [pltpu.make_async_copy(src, dst, sems.at[n]) for n, (src, dst) in enumerate(wanted)]
    for fetch in fetches:
        fetch.start()
    acc[...] = jnp.zeros_like(acc)
    live_m[...] = jnp.zeros_like(live_m)
    cover[1] = jnp.zeros(cover.shape[1:], cover.dtype)
    for fetch in fetches[:6]:
        fetch.wait()

    eye = (lax.broadcasted_iota(jnp.int32, (levels, levels), 0)
           == lax.broadcasted_iota(jnp.int32, (levels, levels), 1))

    def column(ref):
        wide = jnp.broadcast_to(ref[...], (levels, levels))
        return jnp.sum(jnp.where(eye, wide, 0.0), axis=1, keepdims=True)

    lx, ly, tilt, vl = column(lx_ref), column(ly_ref), column(tilt_ref), column(vl_ref)
    ratio = lx / ly
    ilx2 = 1.0 / (lx * lx)
    entries = [tilt * ratio, (1.0 - tilt * tilt) * ratio * ratio, lx * lx]
    for n, entry in enumerate(entries):
        tabs[n] = jnp.broadcast_to(entry[:, :, None], (levels, 8, TILE))
    qtab[0] = jnp.broadcast_to(1.0 / vl, (levels, TILE))
    qtab[1] = jnp.broadcast_to(ilx2 * ilx2, (levels, TILE))

    for fetch in fetches[6:]:
        fetch.wait()
    x0 = sect_ref[0].astype(jnp.float32) * (half_x / GX) + 0.5 / GX
    row = lax.broadcasted_iota(jnp.int32, (TILE, columns), 0)
    lane = lax.broadcasted_iota(jnp.int32, (META, TILE), 1)
    field = lax.broadcasted_iota(jnp.int32, (META, TILE), 0)

    def pack(source, start):
        k = lax.div(source, sources // (2 * REACH + 1)) - REACH
        count = info[source, 3, 0].astype(jnp.int32)
        low = info[source, 3, 1].astype(jnp.int32)
        high = info[source, 3, 2].astype(jnp.int32)
        count = jnp.where((k <= high) & (-k <= low), count, 0)
        shift = lax.rem(start, TILE)
        base = k.astype(jnp.float32) + x0

        def put(t, c):
            first = pl.multiple_of(t * TILE, TILE)
            w = w_all[source, pl.ds(first, TILE), :]
            at = pl.ds(pl.multiple_of(start + first, 16), TILE)
            live_w[at, :] = jnp.where(row < count - first, w.astype(jnp.float32), 0.0)
            m = m_all[source, :, pl.ds(first, TILE)]
            m = pltpu.roll(jnp.where(field == 0, base - m, m), shift, 1)
            here = lax.div(start, TILE) + t
            live_m[here] = jnp.where(lane >= shift, m, live_m[here])
            live_m[here + 1] = jnp.where(lane < shift, m, live_m[here + 1])
            return c

        lax.fori_loop(0, (count + TILE - 1) // TILE, put, 0)
        return start + ((count + 15) // 16) * 16

    total = lax.fori_loop(0, sources, pack, jnp.int32(0))
    live_w[pl.ds(pl.multiple_of(total, 16), chunk), :] = jnp.zeros((chunk, columns), live_w.dtype)
    chunks = (total + chunk - 1) // chunk

    gy = [(lax.broadcasted_iota(jnp.int32, (8, TILE), 0).astype(jnp.float32) + (8 * e + 0.5)) / GY
          for e in range(GY // 8)]
    rises = lax.broadcasted_iota(jnp.int32, (group, TILE), 0)

    def make(slot, block, first_level):
        heights = (rises + first_level).astype(jnp.float32)
        ivl = qtab[0, pl.ds(first_level, group), :]
        scale = qtab[1, pl.ds(first_level, group), :]
        for h in range(parts):
            m = live_m[block * parts + h]
            sep = (heights - m[2:3]) * ivl
            qs = (1.0 + sep * sep) * scale
            xs = [jnp.broadcast_to(m[0:1] + i / GX, (8, TILE)) for i in range(half_x)]
            ys = [g - m[1:2] for g in gy]
            y2s = [y * y for y in ys]
            for r in range(group):
                tv = tabs[0, first_level + r]
                td = tabs[1, first_level + r]
                t0 = tabs[2, first_level + r]
                q = jnp.broadcast_to(qs[r:r + 1], (8, TILE))
                vs = [y * tv for y in ys]
                ds = [y2 * td + t0 for y2 in y2s]
                for i in range(half_x):
                    done = []
                    for v, d in zip(vs, ds):
                        w = xs[i] + v
                        z = w * w + d
                        done.append(pl.reciprocal(z * z * q, approx=True))
                    at = r * half + i * GY
                    cover[slot, h, at:at + GY, :] = jnp.concatenate(done, axis=0)

    def use(slot, block, first_level):
        w = live_w[pl.ds(pl.multiple_of(block * chunk, chunk), chunk), :]
        at = pl.ds(pl.multiple_of(first_level * half, group * half), group * half)
        terms = []
        for h in range(0, parts, 2):
            left = jnp.concatenate([cover[slot, h], cover[slot, h + 1]], axis=1)
            terms.append(jnp.dot(left, w[h * TILE:(h + 2) * TILE],
                                 precision=lax.Precision.DEFAULT,
                                 preferred_element_type=jnp.float32))
        acc[at, :] += sum(terms[1:], terms[0])

    turns = levels // (2 * group)

    def turn(step, c):
        block = lax.div(step, turns)
        level = pl.multiple_of(lax.rem(step, turns) * (2 * group), 2 * group)
        before = jnp.maximum(step - 1, 0)
        use(1, lax.div(before, turns), lax.rem(before, turns) * (2 * group) + group)
        make(0, block, level)
        use(0, block, level)
        make(1, block, level + group)
        return c

    lax.fori_loop(0, chunks * turns, turn, 0)
    use(1, chunks - 1, levels - group)

    share = levels // 2
    sect = sect_ref[0]
    bal = jnp.concatenate([bal_ref[pl.ds(pl.multiple_of(sect * share, share), share), :],
                           bal_ref[pl.ds(pl.multiple_of((1 - sect) * share, share), share), :]],
                          axis=0)
    bal_hi = bal.astype(jnp.bfloat16)
    bal_lo = (bal - bal_hi.astype(jnp.float32)).astype(jnp.bfloat16)
    left = jnp.concatenate([bal_hi, bal_lo], axis=0).astype(jnp.float32)

    def balance(n, c):
        for m in range(4):
            g = n * 8 + m * 2
            a = jnp.concatenate([acc[pl.ds(g + e, levels, stride=half), :] for e in range(2)],
                                axis=1)
            inc = jnp.dot(left, a, precision=lax.Precision.DEFAULT,
                          preferred_element_type=jnp.float32)
            inc = inc[:levels] + inc[levels:]
            for e in range(2):
                at = pl.ds(g + e, share, stride=half)
                mine[at, :] = inc[:share, e * columns:(e + 1) * columns]
                other[at, :] = inc[share:, e * columns:(e + 1) * columns]
        return c

    lax.fori_loop(0, half // 8, balance, 0)
    place = pltpu.make_async_copy(mine.reshape(share, half, columns),
                                  part_ref.at[:, pl.ds(sect * half, half), :], out_sem)
    place.start()
    other_ref[...] = other[...].astype(other_ref.dtype)
    place.wait()


def spread(sect, weights, metas, length_x, length_y, tilt, vert_len, balance):
    slots, sections, rows, columns = weights.shape
    sources = slots * sections
    weights = weights.reshape(sources, rows, columns)
    metas = metas.reshape(sources, META, rows)
    levels = balance.shape[0]
    half_x = GX // sections
    half = half_x * GY
    chunk = 4 * TILE
    live = sources * rows + chunk
    vmem = pl.BlockSpec(memory_space=pltpu.VMEM)
    hbm = pl.BlockSpec(memory_space=pltpu.HBM)
    out = jax.ShapeDtypeStruct((levels // 2 * half, columns), jnp.bfloat16)
    whole = jax.ShapeDtypeStruct((levels // 2, sections * half, columns), jnp.float32)
    line = pltpu.VMEM((1, levels), jnp.float32)
    return pl.pallas_call(
        functools.partial(spread_kernel, levels, half_x),
        out_shape=(whole, out),
        in_specs=[pl.BlockSpec(memory_space=pltpu.SMEM)] + [hbm] * 7,
        out_specs=(hbm, vmem),
        scratch_shapes=[
            pltpu.VMEM((levels * half, columns), jnp.float32),
            pltpu.VMEM((levels // 2 * half, columns), jnp.float32),
            pltpu.VMEM((levels // 2 * half, columns), jnp.float32),
            pltpu.SemaphoreType.DMA,
            pltpu.VMEM((sources, rows, columns), jnp.bfloat16),
            pltpu.VMEM((sources, META, rows), jnp.float32),
            pltpu.SMEM((sources, META, TILE), jnp.float32),
            line, line, line, line,
            pltpu.VMEM((levels, levels), jnp.float32),
            pltpu.VMEM((live, columns), jnp.float32),
            pltpu.VMEM((live // TILE + 1, META, TILE), jnp.float32),
            pltpu.VMEM((2, chunk // TILE, 8 * half, TILE), jnp.float32),
            pltpu.VMEM((3, levels, 8, TILE), jnp.float32),
            pltpu.VMEM((2, levels, TILE), jnp.float32),
            pltpu.SemaphoreType.DMA((8,)),
        ],
        compiler_params=pltpu.CompilerParams(vmem_limit_bytes=VMEM_BYTES),
        name="spread_and_balance",
    )(sect, weights, metas, length_x, length_y, tilt, vert_len, balance)


def shards(blocks, obs_weight, obs_frac, obs_cell, obs_level, obs_count, reach,
           length_x, length_y, tilt, vert_len, balance):
    levels = balance.shape[0]
    columns = obs_weight.shape[3]
    sections = lax.axis_size("sect")
    weights, metas = gather(blocks, obs_weight[0, 0], obs_frac[0, 0], obs_cell[0], obs_level[0],
                            obs_count, reach)
    sect = lax.axis_index("sect").astype(jnp.int32)
    part, other = spread(sect.reshape(1), weights, metas, length_x[None], length_y[None], tilt[None],
                         vert_len[None], balance)
    came = lax.ppermute(other.reshape(levels // sections, -1, columns), "sect", [(0, 1), (1, 0)])
    return lax.dynamic_update_slice(part, came.astype(part.dtype), (0, (1 - sect) * came.shape[1], 0))


def solution(mesh):
    placed = (
        P(("date", "blk"), "sect", None, None),
        P(("date", "blk"), "sect", None, None),
        P(("date", "blk"), "sect", None),
        P(("date", "blk"), "sect", None),
        P(("date", "blk"), "sect"),
        P(("date", "blk"), None),
        P(),
        P(),
        P(),
        P(),
        P(),
    )
    return jax.shard_map(
        functools.partial(shards, mesh.shape["blk"]),
        mesh=mesh,
        in_specs=placed,
        out_specs=P("sect", ("date", "blk"), None),
        check_vma=False,
    )
```
